512 devices in a mesh: seg: 32 (over y, x), head: 16 (over z, core).
Axes of the slice: x: 4, y: 8, z: 8, core: 2. Of those that a mesh axis runs over, the one named last changes fastest.
Arguments:
- queries: bfloat16 [32768, 2048], P(('seg', 'head')), may hold values from -6 to 6
- key_states: bfloat16 [32768, 2048], P(('seg', 'head')), may hold values from -6 to 6
- value_states: bfloat16 [32768, 2048], P(('seg', 'head')), may hold values from -6 to 6
- offsets: int32 [32, 6], P('head'), may hold values from 0 to 31, as said below
Outputs:
- attended: bfloat16 [32768, 2048], P(('seg', 'head'))
The draws below stay inside these ranges and needn't reach their ends.
Inputs may be any that keep to these rules, and one draw needn't show every extreme that they name: offsets[h, l] lies in 0 .. 2^l - 1, and at each level every value of that range is taken by the same number of heads.
All inputs are finite; a program needn't handle non-finite values.
Results may differ from the reference program's by a relative error of at most 0.0044.
Values may be sent and summed in bfloat16 or wider, within the bound.
A program may use at most 64 MiB of HBM per device.

```python
import math
import jax
import jax.numpy as jnp
from jax import lax

D = 2048
H = 32
SEG_ROWS = 1024
SEQ = 32768
LEVELS = 6


def draw_queries(key, part):
    key = jax.random.fold_in(key, 11)
    result = jnp.clip(jax.random.normal(key, (SEQ, D), jnp.float32), -6.0, 6.0)
    return result.astype(jnp.bfloat16)


def draw_key_states(key, part):
    key = jax.random.fold_in(key, 23)
    result = jnp.clip(jax.random.normal(key, (SEQ, D), jnp.float32), -6.0, 6.0)
    return result.astype(jnp.bfloat16)


def draw_offsets(key, part):
    key = jax.random.fold_in(key, 37)
    columns = []
    for level_id in range(LEVELS):
        shuffled = jax.random.permutation(jax.random.fold_in(key, level_id), H)
        columns.append(shuffled.astype(jnp.int32) % 2 ** level_id)
    return jnp.stack(columns, axis=1).astype(jnp.int32)


def block_levels(stream_key, shape, cuts, smallest, high):
    def one(dim, parts):
        draws = jax.random.uniform(jax.random.fold_in(jax.random.fold_in(stream_key, 6), dim), (parts,), jnp.float32, smallest / len(cuts), high / len(cuts))
        return jnp.repeat(jnp.exp(draws), shape[dim] // parts).reshape((-1,) + (1,) * (len(shape) - dim - 1))

    loudness = one(*cuts[0])
    for cut in cuts[1:]:
        loudness = loudness * one(*cut)
    return loudness


def scatter_about(own_key, shape, scale, reach, pieces=(), held_as=jnp.bfloat16):
    gain = block_levels(own_key, shape, pieces, -0.22, 0.18) if pieces else 1.0
    values = jax.random.normal(own_key, shape, jnp.float32) * scale * gain
    return jnp.minimum(jnp.maximum(values, -reach), reach).astype(held_as)


def setup_inputs(seed: int = 0) -> dict:
    seeds = jax.random.split(jax.random.key(seed), 5)
    queries = draw_queries(jax.random.fold_in(seeds[4], 71), 0)
    key_states = draw_key_states(jax.random.fold_in(seeds[4], 71), 0)
    value_states = scatter_about(seeds[2], (SEQ, D), 1.0, 6.0, ((0, 512),))
    offsets = draw_offsets(jax.random.fold_in(seeds[4], 71), 0)
    return {"queries": queries, "key_states": key_states, "value_states": value_states, "offsets": offsets}


def attend_block(query_block, key_block, value_block, score_scale):
    scores = jnp.einsum('qhe,khe->hqk', query_block.astype(jnp.float32), key_block.astype(jnp.float32)) * score_scale
    row_max = lax.optimization_barrier(jnp.max(scores, axis=-1))
    expo = jnp.exp(scores - row_max[..., None])
    denom = lax.optimization_barrier(jnp.sum(expo, axis=-1))
    probs = lax.optimization_barrier(expo.astype(jnp.bfloat16)).astype(jnp.float32)
    summed = jnp.einsum('hqk,khe->hqe', probs, value_block.astype(jnp.float32))
    level_out = summed / denom[..., None]
    lse = row_max + jnp.log(denom)
    return (jnp.transpose(level_out, (1, 0, 2)), jnp.transpose(lse))

def attend_rows(query_rows, key_rows, value_rows, score_scale):
    total = query_rows.shape[0]
    part_count = max(1, total // 512)
    while total % part_count:
        part_count -= 1
    shaped = query_rows.reshape((part_count, total // part_count) + query_rows.shape[1:])
    level_out, lse = lax.map(lambda piece: attend_block(piece, key_rows, value_rows, score_scale), shaped)
    return (level_out.reshape((total,) + level_out.shape[2:]), lse.reshape(total, lse.shape[-1]))

def pick_rows(field, chosen, stride):
    shaped = field.reshape((field.shape[0] // stride, stride) + field.shape[1:])
    return lax.optimization_barrier(jnp.sum(jnp.where(chosen[None, :, :, None], shaped, jnp.zeros_like(shaped)), axis=1))

def reference(queries, key_states, value_states, offsets):
    head_dim = D // H
    score_scale = 1.0 / math.sqrt(head_dim)
    query_all = queries.reshape(SEQ, H, head_dim)
    key_all = key_states.reshape(SEQ, H, head_dim)
    value_all = value_states.reshape(SEQ, H, head_dim)
    for level_id in range(LEVELS):
        stride = 2 ** level_id
        chosen = jnp.arange(stride)[:, None] == offsets[:, level_id][None, :]
        segments = SEQ // (stride * SEG_ROWS)
        query_sel = pick_rows(query_all, chosen, stride).reshape(segments, SEG_ROWS, H, head_dim)
        key_sel = pick_rows(key_all, chosen, stride).reshape(segments, SEG_ROWS, H, head_dim)
        value_sel = pick_rows(value_all, chosen, stride).reshape(segments, SEG_ROWS, H, head_dim)
        level_out, lse = lax.map(lambda group: attend_rows(group[0], group[1], group[2], score_scale), (query_sel, key_sel, value_sel))
        level_out = level_out.reshape(SEQ // stride, H, head_dim)
        lse = lse.reshape(SEQ // stride, H)
        full_out = (level_out[:, None] * chosen[None, :, :, None].astype(jnp.float32)).reshape(SEQ, H, head_dim)
        full_lse = jnp.where(chosen[None], lse[:, None, :], jnp.float32(-jnp.inf)).reshape(SEQ, H)
        if level_id == 0:
            top_lse = full_lse
            weight_sum = jnp.ones_like(full_lse)
            accum = full_out
        else:
            new_top = jnp.maximum(top_lse, full_lse)
            fade = jnp.exp(top_lse - new_top)
            weight = jnp.exp(full_lse - new_top)
            accum = accum * fade[..., None] + weight[..., None] * full_out
            weight_sum = weight_sum * fade + weight
            top_lse = new_top
    return (accum / weight_sum[..., None]).astype(jnp.bfloat16).reshape(SEQ, D)
```

```python
import functools

import jax
import jax.numpy as jnp
from jax import lax
from jax.experimental import pallas as pl
from jax.experimental.pallas import tpu as pltpu
from jax.sharding import PartitionSpec as P

MESH = pl.DeviceIdType.MESH
BF = jnp.bfloat16
F32 = jnp.float32

ROWS = 64
BLOCK = 1024
WIDE = 128
HEADS = 16
NX, NY = 4, 8
Q_AT = {1: 0, 2: 512, 3: 768, 4: 896, 5: 960}
X_AT = {2: 0, 3: 256, 4: 384, 5: 448}
X_ROWS = 480


def rows_of(level):
    return BLOCK >> level


def remote(src, dst, send, recv, seg, head):
    return pltpu.make_async_remote_copy(
        src_ref=src, dst_ref=dst, send_sem=send, recv_sem=recv,
        device_id=(seg, head), device_id_type=MESH,
    )


def drain(ref, sem):
    pltpu.make_async_copy(ref, ref, sem).wait()


def low_lanes(rows):
    return lax.broadcasted_iota(jnp.int32, (rows, WIDE), 1) < WIDE // 2


def dot_t(a, b):
    return lax.dot_general(a, b, (((1,), (1,)), ((), ())), preferred_element_type=F32)


def dot(a, b):
    return lax.dot_general(a, b, (((1,), (0,)), ((), ())), preferred_element_type=F32)


def attend(q, k, v_low, v_high):
    rows = q.shape[0]
    low = low_lanes(rows)
    zero = jnp.zeros_like(q)
    q = q * jnp.asarray(0.125, BF)
    both = jnp.concatenate([jnp.where(low, q, zero), jnp.where(low, zero, q)], axis=0)
    scores = dot_t(both, k)
    top = jnp.max(scores, axis=1, keepdims=True)
    probs = jnp.exp(scores - top).astype(BF)
    first = dot(probs[:rows], v_low)
    second = dot(probs[rows:], v_high)
    total = jnp.where(low, first, second)
    denom = pltpu.roll(jnp.where(low, second, first), WIDE // 2, 1)
    return total, denom, jnp.where(low, top[:rows], top[rows:])


def with_ones(v):
    low = low_lanes(v.shape[0])
    one = jnp.ones_like(v)
    return jnp.where(low, v, one), jnp.where(low, one, v)


def kernel(
    off_ref, q_ref, k_ref, v_ref, out_ref,
    pick, full, own1, got1, gx, gy3, gy4, gy5, qsel, v_one,
    acc, den, top, acc_e, den_e, top_e, merged,
    in_recv, in_send, one_recv, one_send, x_recv, x_send, y_recv, y_send, out_recv, out_send,
):
    seg = lax.axis_index("seg")
    head = lax.axis_index("head")
    x = lax.rem(seg, NX)
    y = lax.div(seg, NX)

    barrier = pltpu.get_barrier_semaphore()

    def greet_head(i, carry):
        pl.semaphore_signal(barrier, inc=1, device_id=(seg, lax.rem(head + i, HEADS)), device_id_type=MESH)
        return carry

    def greet_x(i, carry):
        pl.semaphore_signal(barrier, inc=1, device_id=(y * NX + lax.rem(x + i, NX), head), device_id_type=MESH)
        return carry

    def greet_y(i, carry):
        pl.semaphore_signal(barrier, inc=1, device_id=(lax.rem(y + i, NY) * NX + x, head), device_id_type=MESH)
        return carry

    lax.fori_loop(1, HEADS, greet_head, 0)
    lax.fori_loop(1, NX, greet_x, 0)
    lax.fori_loop(1, NY, greet_y, 0)
    pl.semaphore_wait(barrier, (HEADS - 1) + (NX - 1) + (NY - 1))

    mine = pl.ds(pl.multiple_of(head * ROWS, ROWS), ROWS)
    my_columns = pl.ds(pl.multiple_of(head * WIDE, WIDE), WIDE)
    for a, ref in enumerate((k_ref, v_ref, q_ref)):
        pltpu.make_async_copy(ref.at[:, my_columns], full.at[a, mine], in_recv.at[a]).start()

        def send_in(i, carry, a=a, ref=ref):
            to = lax.rem(head + i, HEADS)
            columns = pl.ds(pl.multiple_of(to * WIDE, WIDE), WIDE)
            remote(ref.at[:, columns], full.at[a, mine], in_send.at[a], in_recv.at[a], seg, to).start()
            return carry

        lax.fori_loop(1, HEADS, send_in, 0)

    r = lax.broadcasted_iota(jnp.int32, (256, 256), 0)
    c = lax.broadcasted_iota(jnp.int32, (256, 256), 1)
    for h in range(2):
        src = jnp.full((256, 256), -1, jnp.int32)
        at = 248
        for level in range(5, 0, -1):
            at -= 256 >> level
            src = jnp.where(r < at + (256 >> level), ((r - at) << level) + off_ref[h, level], src)
        src = jnp.where(r < 248, src, -1)
        pick[h * 256:(h + 1) * 256] = jnp.where(c == src, 1.0, 0.0).astype(BF)

    def select(a):
        low = low_lanes(256)
        pieces = []
        for n in range(4):
            both = dot(pick[...], full[a, n * 256:(n + 1) * 256])
            pieces.append(jnp.where(low, both[:256], both[256:]))
        parts = {}
        at = 0
        for level in range(1, 6):
            step = 256 >> level
            parts[level] = jnp.concatenate([piece[at:at + step] for piece in pieces], axis=0).astype(BF)
            at += step
        return parts

    partner_x = y * NX + (x + 1 - 2 * lax.rem(x, 2))
    partner_y = (y + 1 - 2 * lax.rem(y, 2)) * NX + x

    def start_x(kv):
        parts = select(kv)
        own1[kv] = parts[1]
        for level in range(2, 6):
            gx[kv, x, X_AT[level]:X_AT[level] + rows_of(level)] = parts[level]
        remote(own1.at[kv], got1.at[kv], one_send.at[kv], one_recv.at[kv], partner_x, head).start()

        def send_x(i, carry):
            to = y * NX + lax.rem(x + i, NX)
            remote(gx.at[kv, x], gx.at[kv, x], x_send.at[kv], x_recv.at[kv], to, head).start()
            return carry

        lax.fori_loop(1, NX, send_x, 0)

    def start_y(kv):
        drain(gx.at[kv, pl.ds(0, NX - 1)], x_recv.at[kv])
        for level in range(3, 6):
            rows = rows_of(level)
            src = gx.at[kv, :, pl.ds(X_AT[level], rows)]
            send, recv = y_send.at[level - 3, kv], y_recv.at[level - 3, kv]
            if level == 3:
                remote(src, gy3.at[kv], send, recv, partner_y, head).start()
            else:
                group = 1 << (level - 2)
                base = y - lax.rem(y, group)
                held = gy4 if level == 4 else gy5

                def send_y(i, carry):
                    to = base + lax.rem(y + i, group)
                    remote(src, held.at[kv, group - 1 - i], send, recv, to * NX + x, head).start()
                    return carry

                lax.fori_loop(1, group, send_y, 0)

    drain(full.at[0], in_recv.at[0])
    start_x(0)
    drain(full.at[1], in_recv.at[1])
    start_x(1)
    v_one[0], v_one[1] = with_ones(full[1])
    start_y(0)
    start_y(1)

    drain(full.at[2], in_recv.at[2])
    parts = select(2)
    for level in range(1, 6):
        qsel[Q_AT[level]:Q_AT[level] + rows_of(level)] = parts[level]

    def level_zero(i, carry):
        rows = pl.ds(pl.multiple_of(i * 128, 128), 128)
        acc[rows], den[rows], top[rows] = attend(full[2, rows], full[0], v_one[0], v_one[1])
        return carry

    lax.fori_loop(0, 8, level_zero, 0)

    def keys(level, kv):
        if level == 1:
            return jnp.concatenate([own1[kv], got1[kv]], axis=0)
        rows = rows_of(level)
        near = gx[kv, :, X_AT[level]:X_AT[level] + rows, :].reshape(NX * rows, WIDE)
        if level == 2:
            return near
        far = {3: gy3, 4: gy4, 5: gy5}[level][kv].reshape(BLOCK - NX * rows, WIDE)
        return jnp.concatenate([near, far], axis=0)

    for level in range(1, 6):
        for kv in range(2):
            if level == 1:
                drain(got1.at[kv], one_recv.at[kv])
            elif level >= 3:
                drain({3: gy3, 4: gy4, 5: gy5}[level].at[kv], y_recv.at[level - 3, kv])
        rows, stride = rows_of(level), 1 << level
        k = keys(level, 0)
        v_low, v_high = with_ones(keys(level, 1))
        step = min(rows, 128)
        for n in range(rows // step):
            at = Q_AT[level] + n * step
            found = attend(qsel[at:at + step], k, v_low, v_high)
            for held, value in zip((acc_e, den_e, top_e), found):
                for o in range(stride):
                    held[pl.ds(n * step * stride + o, step, stride=stride), :] = value

        lanes = low_lanes(128)
        offset = jnp.where(lanes, off_ref[0, level], off_ref[1, level])

        def merge(i, carry):
            part = pl.ds(pl.multiple_of(i * 128, 128), 128)
            t = lax.broadcasted_iota(jnp.int32, (128, WIDE), 0)
            chosen = (t & (stride - 1)) == offset
            level_top = jnp.where(chosen, top_e[part], -jnp.inf)
            old = top[part]
            new = jnp.maximum(old, level_top)
            fade, weight = jnp.exp(old - new), jnp.exp(level_top - new)
            acc[part] = acc[part] * fade + weight * acc_e[part]
            den[part] = den[part] * fade + weight * den_e[part]
            top[part] = new
            return carry

        lax.fori_loop(0, 8, merge, 0)

    def finish(i, carry):
        part = pl.ds(pl.multiple_of(i * 128, 128), 128)
        merged[part] = (acc[part] / den[part]).astype(BF)
        return carry

    lax.fori_loop(0, 8, finish, 0)
    pltpu.make_async_copy(merged.at[mine], out_ref.at[:, my_columns], out_recv).start()

    def send_out(i, carry):
        to = lax.rem(head + i, HEADS)
        part = pl.ds(pl.multiple_of(to * ROWS, ROWS), ROWS)
        remote(merged.at[part], out_ref.at[:, my_columns], out_send, out_recv, seg, to).start()
        return carry

    lax.fori_loop(1, HEADS, send_out, 0)

    others = pl.ds(0, BLOCK - ROWS)
    for a in range(3):
        drain(full.at[a, others], in_send.at[a])
    for kv in range(2):
        drain(own1.at[kv], one_send.at[kv])
        drain(gx.at[kv, pl.ds(0, NX - 1)], x_send.at[kv])
        for n, held in enumerate((gy3, gy4, gy5)):
            drain(held.at[kv], y_send.at[n, kv])
    drain(merged.at[others], out_send)
    drain(out_ref, out_recv)


def per_device(queries, key_states, value_states, offsets):
    dma = pltpu.SemaphoreType.DMA
    anywhere = pl.BlockSpec(memory_space=pl.ANY)
    return pl.pallas_call(
        kernel,
        out_shape=jax.ShapeDtypeStruct(queries.shape, BF),
        in_specs=[pl.BlockSpec(memory_space=pltpu.SMEM)] + [anywhere] * 3,
        out_specs=anywhere,
        scratch_shapes=[
            pltpu.VMEM((512, 256), BF),
            pltpu.VMEM((3, BLOCK, WIDE), BF),
            pltpu.VMEM((2, 512, WIDE), BF),
            pltpu.VMEM((2, 512, WIDE), BF),
            pltpu.VMEM((2, NX, X_ROWS, WIDE), BF),
            pltpu.VMEM((2, NX, 128, WIDE), BF),
            pltpu.VMEM((2, 3, NX, 64, WIDE), BF),
            pltpu.VMEM((2, 7, NX, 32, WIDE), BF),
            pltpu.VMEM((992, WIDE), BF),
            pltpu.VMEM((2, BLOCK, WIDE), BF),
        ] + [pltpu.VMEM((BLOCK, WIDE), F32)] * 6 + [
            pltpu.VMEM((BLOCK, WIDE), BF),
            dma((3,)), dma((3,)), dma((2,)), dma((2,)), dma((2,)), dma((2,)),
            dma((3, 2)), dma((3, 2)), dma, dma,
        ],
        compiler_params=pltpu.CompilerParams(
            collective_id=0, has_side_effects=True, vmem_limit_bytes=48 * 1024 * 1024
        ),
        cost_estimate=pl.CostEstimate(flops=1100000000, bytes_accessed=1100000, transcendentals=4200000),
    )(offsets, queries, key_states, value_states)


def solution(mesh):
    rows = P(("seg", "head"), None)
    return jax.shard_map(
        per_device, mesh=mesh, in_specs=(rows, rows, rows, P("head", None)), out_specs=rows, check_vma=False
    )
```

```python
import jax
import jax.numpy as jnp
from jax import lax
from jax.experimental import pallas as pl
from jax.experimental.pallas import tpu as pltpu
from jax.sharding import PartitionSpec as P

MESH = pl.DeviceIdType.MESH
BF = jnp.bfloat16
F32 = jnp.float32

ROWS = 64
BLOCK = 1024
WIDE = 128
HEADS = 16
NX, NY = 4, 8
Q_AT = {1: 0, 2: 512, 3: 768, 4: 896, 5: 960}
UP_AT = {3: 0, 4: 128, 5: 192}
UP_ROWS = 224
COLUMN_KEYS = 256
STAT_ROWS = 32
STAT_GROUPS = UP_ROWS // STAT_ROWS


def rows_of(level):
    return BLOCK >> level


def remote(src, dst, send, recv, seg, head):
    return pltpu.make_async_remote_copy(
        src_ref=src, dst_ref=dst, send_sem=send, recv_sem=recv,
        device_id=(seg, head), device_id_type=MESH,
    )


def drain(ref, sem):
    pltpu.make_async_copy(ref, ref, sem).wait()


def lanes_of(rows):
    return lax.broadcasted_iota(jnp.int32, (rows, WIDE), 1)


def low_lanes(rows):
    return lanes_of(rows) < WIDE // 2


def dot_t(a, b):
    return lax.dot_general(a, b, (((1,), (1,)), ((), ())), preferred_element_type=F32)


def dot(a, b):
    return lax.dot_general(a, b, (((1,), (0,)), ((), ())), preferred_element_type=F32)


def attend(q, k, v_low, v_high):
    rows = q.shape[0]
    low = low_lanes(rows)
    zero = jnp.zeros_like(q)
    q = q * jnp.asarray(0.125, BF)
    both = jnp.concatenate([jnp.where(low, q, zero), jnp.where(low, zero, q)], axis=0)
    scores = dot_t(both, k)
    top = jnp.max(scores, axis=1, keepdims=True)
    probs = jnp.exp(scores - top).astype(BF)
    first = dot(probs[:rows], v_low)
    second = dot(probs[rows:], v_high)
    total = jnp.where(low, first, second)
    denom = pltpu.roll(jnp.where(low, second, first), WIDE // 2, 1)
    return total, denom, jnp.where(low, top[:rows], top[rows:])


def with_ones(v):
    low = low_lanes(v.shape[0])
    one = jnp.ones_like(v)
    return jnp.where(low, v, one), jnp.where(low, one, v)


def kernel(
    off_hbm, q_ref, k_ref, v_ref, out_ref,
    off_ref, pick, full, own1, got1, gx, yk, qsel, qx, part_o, part_s, back_o, back_s, v_one,
    acc, den, top, acc_e, den_e, top_e, merged,
    off_sem, in_recv, in_send, one_recv, one_send, x_recv, x_send, y_recv, y_send,
    q_recv, q_send, back_recv, back_send, out_recv, out_send,
):
    seg = lax.axis_index("seg")
    head = lax.axis_index("head")
    x = lax.rem(seg, NX)
    y = lax.div(seg, NX)
    offsets = pltpu.make_async_copy(off_hbm, off_ref, off_sem)
    offsets.start()

    barrier = pltpu.get_barrier_semaphore()

    def at_x(i):
        return y * NX + lax.rem(x + i, NX)

    def greet_head(i, carry):
        pl.semaphore_signal(barrier, inc=1, device_id=(seg, lax.rem(head + i, HEADS)), device_id_type=MESH)
        return carry

    def greet_x(i, carry):
        pl.semaphore_signal(barrier, inc=1, device_id=(at_x(i), head), device_id_type=MESH)
        return carry

    def greet_y(i, carry):
        pl.semaphore_signal(barrier, inc=1, device_id=(lax.rem(y + i, NY) * NX + x, head), device_id_type=MESH)
        return carry

    lax.fori_loop(1, HEADS, greet_head, 0)
    lax.fori_loop(1, NX, greet_x, 0)
    lax.fori_loop(1, NY, greet_y, 0)
    pl.semaphore_wait(barrier, (HEADS - 1) + (NX - 1) + (NY - 1))

    mine = pl.ds(pl.multiple_of(head * ROWS, ROWS), ROWS)
    others = pl.ds(0, BLOCK - ROWS)
    my_columns = pl.ds(pl.multiple_of(head * WIDE, WIDE), WIDE)

    def exchange(a):
        ref = (k_ref, v_ref, q_ref)[a]

        def send_in(i, carry):
            to = lax.rem(head + i, HEADS)
            columns = pl.ds(pl.multiple_of(to * WIDE, WIDE), WIDE)
            remote(ref.at[:, columns], full.at[a, mine], in_send.at[a], in_recv.at[a], seg, to).start()
            return carry

        lax.fori_loop(1, HEADS, send_in, 0)
        pltpu.make_async_copy(ref.at[:, my_columns], full.at[a, mine], in_recv.at[a]).start()

    exchange(0)

    offsets.wait()
    r = lax.broadcasted_iota(jnp.int32, (256, 256), 0)
    c = lax.broadcasted_iota(jnp.int32, (256, 256), 1)
    for h in range(2):
        src = jnp.full((256, 256), -1, jnp.int32)
        at = 248
        for level in range(5, 0, -1):
            at -= 256 >> level
            src = jnp.where(r < at + (256 >> level), ((r - at) << level) + off_ref[h, level], src)
        src = jnp.where(r < 248, src, -1)
        pick[h * 256:(h + 1) * 256] = jnp.where(c == src, 1.0, 0.0).astype(BF)

    def select(a):
        low = low_lanes(256)
        pieces = []
        for n in range(4):
            both = dot(pick[...], full[a, n * 256:(n + 1) * 256])
            pieces.append(jnp.where(low, both[:256], both[256:]))
        parts = {}
        at = 0
        for level in range(1, 6):
            step = 256 >> level
            parts[level] = jnp.concatenate([piece[at:at + step] for piece in pieces], axis=0).astype(BF)
            at += step
        return parts

    partner_x = y * NX + (x + 1 - 2 * lax.rem(x, 2))

    def start_levels(kv):
        parts = select(kv)
        for level in range(3, 6):
            group = 1 << (level - 2)
            rows = rows_of(level)
            place = lax.rem(y, group)
            slot = yk.at[kv, level - 3, pl.ds(pl.multiple_of(place * rows, rows), rows)]
            slot[...] = parts[level]

            def send_y(i, carry):
                to = y - place + lax.rem(place + i, group)
                remote(slot, slot, y_send.at[kv, level - 3], y_recv.at[kv, level - 3], to * NX + x, head).start()
                return carry

            lax.fori_loop(1, group, send_y, 0)
        own1[kv] = parts[1]
        gx[kv, x] = parts[2]
        remote(own1.at[kv], got1.at[kv], one_send.at[kv], one_recv.at[kv], partner_x, head).start()

        def send_x(i, carry):
            remote(gx.at[kv, x], gx.at[kv, x], x_send.at[kv], x_recv.at[kv], at_x(i), head).start()
            return carry

        lax.fori_loop(1, NX, send_x, 0)

    drain(full.at[0, others], in_send.at[0])
    exchange(1)
    drain(full.at[0], in_recv.at[0])
    start_levels(0)
    drain(full.at[1, others], in_send.at[1])
    exchange(2)
    drain(full.at[1], in_recv.at[1])
    start_levels(1)
    v_one[0], v_one[1] = with_ones(full[1])

    drain(full.at[2], in_recv.at[2])
    parts = select(2)
    for level in range(3, 6):
        qx[x, UP_AT[level]:UP_AT[level] + rows_of(level)] = parts[level]

    def send_q(i, carry):
        remote(qx.at[x], qx.at[x], q_send, q_recv, at_x(i), head).start()
        return carry

    lax.fori_loop(1, NX, send_q, 0)
    for level in range(1, 3):
        qsel[Q_AT[level]:Q_AT[level] + rows_of(level)] = parts[level]

    def level_zero(i, carry):
        rows = pl.ds(pl.multiple_of(i * 128, 128), 128)
        acc[rows], den[rows], top[rows] = attend(full[2, rows], full[0], v_one[0], v_one[1])
        return carry

    lax.fori_loop(0, 8, level_zero, 0)

    drain(qx.at[pl.ds(0, NX - 1)], q_recv)
    group_lane = lax.rem(lanes_of(STAT_ROWS), WIDE // 2) // 8
    stats = [jnp.zeros((STAT_ROWS, WIDE), F32) for _ in range(NX)]
    for level in range(3, 6):
        rows = rows_of(level)
        for kv in range(2):
            drain(yk.at[kv, level - 3, pl.ds(0, COLUMN_KEYS - rows)], y_recv.at[kv, level - 3])
        at = UP_AT[level]
        v_low, v_high = with_ones(yk[1, level - 3])
        for n in range(NX):
            total, denom, peak = attend(qx[n, at:at + rows], yk[0, level - 3], v_low, v_high)
            part_o[n, at:at + rows] = (total / denom).astype(BF)
            lse = peak + jnp.log(denom)
            for m in range(rows // STAT_ROWS):
                stats[n] = jnp.where(
                    group_lane == at // STAT_ROWS + m, lse[m * STAT_ROWS:(m + 1) * STAT_ROWS], stats[n]
                )
    for n in range(NX):
        part_s[n] = stats[n]
    back_o[x] = part_o[x]
    back_s[x] = part_s[x]

    def send_back(i, carry):
        to = lax.rem(x + i, NX)
        remote(part_o.at[to], back_o.at[x], back_send.at[0], back_recv.at[0], at_x(i), head).start()
        remote(part_s.at[to], back_s.at[x], back_send.at[1], back_recv.at[1], at_x(i), head).start()
        return carry

    lax.fori_loop(1, NX, send_back, 0)

    def spread(at, stride, values):
        for held, value in zip((acc_e, den_e, top_e), values):
            for o in range(stride):
                held[pl.ds(at * stride + o, value.shape[0], stride=stride), :] = value

    def merge_level(level):
        stride = 1 << level
        offset = jnp.where(low_lanes(128), off_ref[0, level], off_ref[1, level])

        def merge(i, carry):
            part = pl.ds(pl.multiple_of(i * 128, 128), 128)
            t = lax.broadcasted_iota(jnp.int32, (128, WIDE), 0)
            chosen = (t & (stride - 1)) == offset
            level_top = jnp.where(chosen, top_e[part], -jnp.inf)
            old = top[part]
            new = jnp.maximum(old, level_top)
            fade, weight = jnp.exp(old - new), jnp.exp(level_top - new)
            acc[part] = acc[part] * fade + weight * acc_e[part]
            den[part] = den[part] * fade + weight * den_e[part]
            top[part] = new
            return carry

        lax.fori_loop(0, 8, merge, 0)

    for level in range(1, 3):
        for kv in range(2):
            if level == 1:
                drain(got1.at[kv], one_recv.at[kv])
            else:
                drain(gx.at[kv, pl.ds(0, NX - 1)], x_recv.at[kv])
        if level == 1:
            k, v = (jnp.concatenate([own1[kv], got1[kv]], axis=0) for kv in range(2))
        else:
            k, v = (gx[kv].reshape(BLOCK, WIDE) for kv in range(2))
        v_low, v_high = with_ones(v)
        for n in range(rows_of(level) // 128):
            at = Q_AT[level] + n * 128
            spread(n * 128, 1 << level, attend(qsel[at:at + 128], k, v_low, v_high))
        merge_level(level)

    drain(back_o.at[pl.ds(0, NX - 1)], back_recv.at[0])
    drain(back_s.at[pl.ds(0, NX - 1)], back_recv.at[1])
    low = low_lanes(STAT_ROWS)
    for level in range(3, 6):
        for m in range(rows_of(level) // STAT_ROWS):
            at = UP_AT[level] + m * STAT_ROWS
            lses = []
            for n in range(NX):
                here = jnp.where(group_lane == at // STAT_ROWS, back_s[n], -jnp.inf)
                lses.append(jnp.where(
                    low,
                    jnp.max(jnp.where(low, here, -jnp.inf), axis=1, keepdims=True),
                    jnp.max(jnp.where(low, -jnp.inf, here), axis=1, keepdims=True),
                ))
            peak = jnp.maximum(jnp.maximum(lses[0], lses[1]), jnp.maximum(lses[2], lses[3]))
            weights = [jnp.exp(lse - peak) for lse in lses]
            total = sum(w * back_o[n, at:at + STAT_ROWS].astype(F32) for n, w in enumerate(weights))
            spread(m * STAT_ROWS, 1 << level, (total, sum(weights), peak))
        merge_level(level)

    def finish(i, carry):
        part = pl.ds(pl.multiple_of(i * 128, 128), 128)
        merged[part] = (acc[part] / den[part]).astype(BF)
        return carry

    lax.fori_loop(0, 8, finish, 0)

    def send_out(i, carry):
        to = lax.rem(head + i, HEADS)
        part = pl.ds(pl.multiple_of(to * ROWS, ROWS), ROWS)
        remote(merged.at[part], out_ref.at[:, my_columns], out_send, out_recv, seg, to).start()
        return carry

    lax.fori_loop(1, HEADS, send_out, 0)
    pltpu.make_async_copy(merged.at[mine], out_ref.at[:, my_columns], out_recv).start()

    drain(full.at[2, others], in_send.at[2])
    for kv in range(2):
        drain(own1.at[kv], one_send.at[kv])
        drain(gx.at[kv, pl.ds(0, NX - 1)], x_send.at[kv])
        for level in range(3, 6):
            drain(yk.at[kv, level - 3, pl.ds(0, COLUMN_KEYS - rows_of(level))], y_send.at[kv, level - 3])
    drain(qx.at[pl.ds(0, NX - 1)], q_send)
    drain(back_o.at[pl.ds(0, NX - 1)], back_send.at[0])
    drain(back_s.at[pl.ds(0, NX - 1)], back_send.at[1])
    drain(merged.at[others], out_send)
    drain(out_ref, out_recv)


def per_device(queries, key_states, value_states, offsets):
    dma = pltpu.SemaphoreType.DMA
    hbm = pl.BlockSpec(memory_space=pltpu.HBM)
    return pl.pallas_call(
        kernel,
        out_shape=jax.ShapeDtypeStruct(queries.shape, BF),
        in_specs=[hbm] * 4,
        out_specs=pl.BlockSpec(memory_space=pl.ANY),
        scratch_shapes=[
            pltpu.SMEM((2, 6), jnp.int32),
            pltpu.VMEM((512, 256), BF),
            pltpu.VMEM((3, BLOCK, WIDE), BF),
            pltpu.VMEM((2, 512, WIDE), BF),
            pltpu.VMEM((2, 512, WIDE), BF),
            pltpu.VMEM((2, NX, 256, WIDE), BF),
            pltpu.VMEM((2, 3, COLUMN_KEYS, WIDE), BF),
            pltpu.VMEM((768, WIDE), BF),
            pltpu.VMEM((NX, UP_ROWS, WIDE), BF),
            pltpu.VMEM((NX, UP_ROWS, WIDE), BF),
            pltpu.VMEM((NX, STAT_ROWS, WIDE), F32),
            pltpu.VMEM((NX, UP_ROWS, WIDE), BF),
            pltpu.VMEM((NX, STAT_ROWS, WIDE), F32),
            pltpu.VMEM((2, BLOCK, WIDE), BF),
        ] + [pltpu.VMEM((BLOCK, WIDE), F32)] * 6 + [
            pltpu.VMEM((BLOCK, WIDE), BF),
            dma, dma((3,)), dma((3,)), dma((2,)), dma((2,)), dma((2,)), dma((2,)), dma((2, 3)), dma((2, 3)),
            dma, dma, dma((2,)), dma((2,)), dma, dma,
        ],
        compiler_params=pltpu.CompilerParams(
            collective_id=0, has_side_effects=True, vmem_limit_bytes=48 * 1024 * 1024
        ),
        cost_estimate=pl.CostEstimate(flops=1100000000, bytes_accessed=1100000, transcendentals=4200000),
    )(*(pltpu.with_memory_space_constraint(a, pltpu.HBM) for a in (offsets, queries, key_states, value_states)))


def solution(mesh):
    rows = P(("seg", "head"), None)
    return jax.shard_map(
        per_device, mesh=mesh, in_specs=(rows, rows, rows, P("head", None)), out_specs=rows, check_vma=False
    )
```

```python
import jax
import jax.numpy as jnp
from jax import lax
from jax.experimental import pallas as pl
from jax.experimental.pallas import tpu as pltpu
from jax.sharding import PartitionSpec as P

MESH = pl.DeviceIdType.MESH
BF = jnp.bfloat16
F32 = jnp.float32

ROWS = 64
BLOCK = 1024
WIDE = 128
HEADS = 16
D = 2048
NX, NY = 4, 8
Q_AT = {1: 0, 2: 512, 3: 768, 4: 896, 5: 960}
UP_AT = {3: 0, 4: 128, 5: 192}
UP_ROWS = 224
COLUMN_KEYS = 256
STAT_ROWS = 32
STAT_GROUPS = UP_ROWS // STAT_ROWS


def rows_of(level):
    return BLOCK >> level


def remote(src, dst, send, recv, seg, head):
    return pltpu.make_async_remote_copy(
        src_ref=src, dst_ref=dst, send_sem=send, recv_sem=recv,
        device_id=(seg, head), device_id_type=MESH,
    )


def drain(ref, sem):
    pltpu.make_async_copy(ref, ref, sem).wait()


def lanes_of(rows):
    return lax.broadcasted_iota(jnp.int32, (rows, WIDE), 1)


def low_lanes(rows):
    return lanes_of(rows) < WIDE // 2


def dot_t(a, b):
    return lax.dot_general(a, b, (((1,), (1,)), ((), ())), preferred_element_type=F32)


def dot(a, b):
    return lax.dot_general(a, b, (((1,), (0,)), ((), ())), preferred_element_type=F32)


def attend(q, k, v_low, v_high):
    rows = q.shape[0]
    low = low_lanes(rows)
    zero = jnp.zeros_like(q)
    q = q * jnp.asarray(0.125, BF)
    both = jnp.concatenate([jnp.where(low, q, zero), jnp.where(low, zero, q)], axis=0)
    scores = dot_t(both, k)
    top = jnp.max(scores, axis=1, keepdims=True)
    probs = jnp.exp(scores - top).astype(BF)
    first = dot(probs[:rows], v_low)
    second = dot(probs[rows:], v_high)
    total = jnp.where(low, first, second)
    denom = pltpu.roll(jnp.where(low, second, first), WIDE // 2, 1)
    return total, denom, jnp.where(low, top[:rows], top[rows:])


def with_ones(v):
    low = low_lanes(v.shape[0])
    one = jnp.ones_like(v)
    return jnp.where(low, v, one), jnp.where(low, one, v)


def kernel(
    off_hbm, q_ref, k_ref, v_ref, out_ref,
    off_ref, off_tiles, pick, pick_up, full, own1, got1, gx, yk, qsel, qx, part_o, part_s, back_o, back_s, v_one,
    acc, den, top, acc_e, den_e, top_e, up_o, up_d, up_t, merged, final, early, late, late_in, placed,
    off_sem, off_recv, off_send, in_recv, in_send, one_recv, one_send, x_recv, x_send, y_recv, y_send,
    q_recv, q_send, back_recv, back_send, early_recv, early_send, late_recv, late_send, out_sem,
):
    seg = lax.axis_index("seg")
    head = lax.axis_index("head")
    x = lax.rem(seg, NX)
    y = lax.div(seg, NX)
    offsets = pltpu.make_async_copy(off_hbm, off_ref, off_sem)
    offsets.start()

    barrier = pltpu.get_barrier_semaphore()

    def at_x(i):
        return y * NX + lax.rem(x + i, NX)

    def greet_head(i, carry):
        pl.semaphore_signal(barrier, inc=1, device_id=(seg, lax.rem(head + i, HEADS)), device_id_type=MESH)
        return carry

    def greet_x(i, carry):
        pl.semaphore_signal(barrier, inc=1, device_id=(at_x(i), head), device_id_type=MESH)
        return carry

    def greet_y(i, carry):
        pl.semaphore_signal(barrier, inc=1, device_id=(lax.rem(y + i, NY) * NX + x, head), device_id_type=MESH)
        return carry

    lax.fori_loop(1, HEADS, greet_head, 0)
    lax.fori_loop(1, NX, greet_x, 0)
    lax.fori_loop(1, NY, greet_y, 0)
    pl.semaphore_wait(barrier, (HEADS - 1) + (NX - 1) + (NY - 1))

    mine = pl.ds(pl.multiple_of(head * ROWS, ROWS), ROWS)
    others = pl.ds(0, BLOCK - ROWS)
    my_columns = pl.ds(pl.multiple_of(head * WIDE, WIDE), WIDE)

    def exchange(a):
        ref = (k_ref, v_ref, q_ref)[a]

        def send_in(i, carry):
            to = lax.rem(head + i, HEADS)
            columns = pl.ds(pl.multiple_of(to * WIDE, WIDE), WIDE)
            remote(ref.at[:, columns], full.at[a, mine], in_send.at[a], in_recv.at[a], seg, to).start()
            return carry

        lax.fori_loop(1, HEADS, send_in, 0)
        pltpu.make_async_copy(ref.at[:, my_columns], full.at[a, mine], in_recv.at[a]).start()

    exchange(0)

    offsets.wait()
    level_row = lax.broadcasted_iota(jnp.int32, (8, WIDE), 0)
    tile = jnp.zeros((8, WIDE), jnp.int32)
    for level in range(1, 6):
        tile = jnp.where(level_row == level, jnp.where(low_lanes(8), off_ref[0, level], off_ref[1, level]), tile)
    off_tiles[head] = tile

    def send_offsets(i, carry):
        to = lax.rem(head + i, HEADS)
        remote(off_tiles.at[head], off_tiles.at[head], off_send, off_recv, seg, to).start()
        return carry

    lax.fori_loop(1, HEADS, send_offsets, 0)

    r = lax.broadcasted_iota(jnp.int32, (256, 256), 0)
    c = lax.broadcasted_iota(jnp.int32, (256, 256), 1)
    for h in range(2):
        src = jnp.full((256, 256), -1, jnp.int32)
        at = 248
        for level in range(5, 0, -1):
            at -= 256 >> level
            src = jnp.where(r < at + (256 >> level), ((r - at) << level) + off_ref[h, level], src)
        src = jnp.where(r < 248, src, -1)
        pick[h * 256:(h + 1) * 256] = jnp.where(c == src, 1.0, 0.0).astype(BF)

    r = lax.broadcasted_iota(jnp.int32, (64, 256), 0)
    c = lax.broadcasted_iota(jnp.int32, (64, 256), 1)
    for h in range(2):
        j = r & 15
        src = jnp.where(
            j < 8, (j << 3) + off_ref[h, 3],
            jnp.where(j < 12, ((j - 8) << 4) + off_ref[h, 4], ((j - 12) << 5) + off_ref[h, 5]),
        ) + ((r >> 4) << 6)
        pick_up[h * 64:(h + 1) * 64] = jnp.where((c == src) & (j < 14), 1.0, 0.0).astype(BF)

    def select(a):
        low = low_lanes(256)
        pieces = []
        for n in range(4):
            both = dot(pick[...], full[a, n * 256:(n + 1) * 256])
            pieces.append(jnp.where(low, both[:256], both[256:]))
        parts = {}
        at = 0
        for level in range(1, 6):
            step = 256 >> level
            parts[level] = jnp.concatenate([piece[at:at + step] for piece in pieces], axis=0).astype(BF)
            at += step
        return parts

    partner_x = y * NX + (x + 1 - 2 * lax.rem(x, 2))

    def start_levels(kv):
        parts = select(kv)
        for level in range(3, 6):
            group = 1 << (level - 2)
            rows = rows_of(level)
            place = lax.rem(y, group)
            slot = yk.at[kv, level - 3, pl.ds(pl.multiple_of(place * rows, rows), rows)]
            slot[...] = parts[level]

            def send_y(i, carry):
                to = y - place + lax.rem(place + i, group)
                remote(slot, slot, y_send.at[kv, level - 3], y_recv.at[kv, level - 3], to * NX + x, head).start()
                return carry

            lax.fori_loop(1, group, send_y, 0)
        own1[kv] = parts[1]
        gx[kv, x] = parts[2]
        remote(own1.at[kv], got1.at[kv], one_send.at[kv], one_recv.at[kv], partner_x, head).start()

        def send_x(i, carry):
            remote(gx.at[kv, x], gx.at[kv, x], x_send.at[kv], x_recv.at[kv], at_x(i), head).start()
            return carry

        lax.fori_loop(1, NX, send_x, 0)

    drain(full.at[0, others], in_send.at[0])
    exchange(1)
    drain(full.at[0], in_recv.at[0])
    start_levels(0)
    drain(full.at[1, others], in_send.at[1])
    exchange(2)
    drain(full.at[1], in_recv.at[1])
    start_levels(1)
    v_one[0], v_one[1] = with_ones(full[1])

    drain(full.at[2], in_recv.at[2])
    parts = select(2)
    for level in range(3, 6):
        qx[x, UP_AT[level]:UP_AT[level] + rows_of(level)] = parts[level]

    def send_q(i, carry):
        remote(qx.at[x], qx.at[x], q_send, q_recv, at_x(i), head).start()
        return carry

    lax.fori_loop(1, NX, send_q, 0)
    for level in range(1, 3):
        qsel[Q_AT[level]:Q_AT[level] + rows_of(level)] = parts[level]

    def level_zero(i, carry):
        rows = pl.ds(pl.multiple_of(i * 128, 128), 128)
        acc[rows], den[rows], top[rows] = attend(full[2, rows], full[0], v_one[0], v_one[1])
        return carry

    lax.fori_loop(0, 8, level_zero, 0)

    drain(qx.at[pl.ds(0, NX - 1)], q_recv)
    group_lane = lax.rem(lanes_of(STAT_ROWS), WIDE // 2) // 8
    stats = [jnp.zeros((STAT_ROWS, WIDE), F32) for _ in range(NX)]
    for level in range(3, 6):
        rows = rows_of(level)
        for kv in range(2):
            drain(yk.at[kv, level - 3, pl.ds(0, COLUMN_KEYS - rows)], y_recv.at[kv, level - 3])
        at = UP_AT[level]
        v_low, v_high = with_ones(yk[1, level - 3])
        for n in range(NX):
            total, denom, peak = attend(qx[n, at:at + rows], yk[0, level - 3], v_low, v_high)
            part_o[n, at:at + rows] = (total / denom).astype(BF)
            lse = peak + jnp.log(denom)
            for m in range(rows // STAT_ROWS):
                stats[n] = jnp.where(
                    group_lane == at // STAT_ROWS + m, lse[m * STAT_ROWS:(m + 1) * STAT_ROWS], stats[n]
                )
    for n in range(NX):
        part_s[n] = stats[n]
    back_o[x] = part_o[x]
    back_s[x] = part_s[x]

    def send_back(i, carry):
        to = lax.rem(x + i, NX)
        remote(part_o.at[to], back_o.at[x], back_send.at[0], back_recv.at[0], at_x(i), head).start()
        remote(part_s.at[to], back_s.at[x], back_send.at[1], back_recv.at[1], at_x(i), head).start()
        return carry

    lax.fori_loop(1, NX, send_back, 0)

    def spread(at, stride, values):
        for held, value in zip((acc_e, den_e, top_e), values):
            for o in range(stride):
                held[pl.ds(at * stride + o, value.shape[0], stride=stride), :] = value

    def merge_level(level):
        stride = 1 << level
        offset = jnp.where(low_lanes(128), off_ref[0, level], off_ref[1, level])

        def merge(i, carry):
            part = pl.ds(pl.multiple_of(i * 128, 128), 128)
            t = lax.broadcasted_iota(jnp.int32, (128, WIDE), 0)
            chosen = (t & (stride - 1)) == offset
            level_top = jnp.where(chosen, top_e[part], -jnp.inf)
            old = top[part]
            new = jnp.maximum(old, level_top)
            fade, weight = jnp.exp(old - new), jnp.exp(level_top - new)
            acc[part] = acc[part] * fade + weight * acc_e[part]
            den[part] = den[part] * fade + weight * den_e[part]
            top[part] = new
            return carry

        lax.fori_loop(0, 8, merge, 0)

    for level in range(1, 3):
        for kv in range(2):
            if level == 1:
                drain(got1.at[kv], one_recv.at[kv])
            else:
                drain(gx.at[kv, pl.ds(0, NX - 1)], x_recv.at[kv])
        if level == 1:
            k, v = (jnp.concatenate([own1[kv], got1[kv]], axis=0) for kv in range(2))
        else:
            k, v = (gx[kv].reshape(BLOCK, WIDE) for kv in range(2))
        v_low, v_high = with_ones(v)
        for n in range(rows_of(level) // 128):
            at = Q_AT[level] + n * 128
            spread(n * 128, 1 << level, attend(qsel[at:at + 128], k, v_low, v_high))
        merge_level(level)

    def finish(i, carry):
        part = pl.ds(pl.multiple_of(i * 128, 128), 128)
        merged[part] = (acc[part] / den[part]).astype(BF)
        return carry

    lax.fori_loop(0, 8, finish, 0)

    def send_early(i, carry):
        to = lax.rem(head + i, HEADS)
        part = pl.ds(pl.multiple_of(to * ROWS, ROWS), ROWS)
        remote(merged.at[part], early.at[:, my_columns], early_send, early_recv, seg, to).start()
        return carry

    lax.fori_loop(1, HEADS, send_early, 0)
    pltpu.make_async_copy(merged.at[mine], early.at[:, my_columns], early_recv).start()

    drain(back_o.at[pl.ds(0, NX - 1)], back_recv.at[0])
    drain(back_s.at[pl.ds(0, NX - 1)], back_recv.at[1])
    low = low_lanes(STAT_ROWS)
    for m in range(STAT_GROUPS):
        rows = pl.ds(m * STAT_ROWS, STAT_ROWS)
        lses = []
        for n in range(NX):
            here = jnp.where(group_lane == m, back_s[n], -jnp.inf)
            lses.append(jnp.where(
                low,
                jnp.max(jnp.where(low, here, -jnp.inf), axis=1, keepdims=True),
                jnp.max(jnp.where(low, -jnp.inf, here), axis=1, keepdims=True),
            ))
        peak = jnp.maximum(jnp.maximum(lses[0], lses[1]), jnp.maximum(lses[2], lses[3]))
        weights = [jnp.exp(lse - peak) for lse in lses]
        up_o[rows] = sum(w * back_o[n, rows].astype(F32) for n, w in enumerate(weights))
        up_d[rows] = sum(weights)
        up_t[rows] = peak

    def merge_up(i, carry):
        held = []
        for level in range(3, 6):
            count = 256 >> level
            at = pl.ds(pl.multiple_of(UP_AT[level] + i * count, 8), count)
            held.append((level, up_o[at], up_d[at], up_t[at]))
        t = lax.broadcasted_iota(jnp.int32, (32, WIDE), 0)
        for n in range(8):
            part = pl.ds(pl.multiple_of(i * 256 + n * 32, 32), 32)
            total, denom, peak = acc[part], den[part], top[part]
            for level, *compact in held:
                stride = 1 << level
                count = 32 >> level
                o, d, p = (
                    jnp.concatenate([
                        jnp.broadcast_to(v[n * count + k:n * count + k + 1], (stride, WIDE)) for k in range(count)
                    ], axis=0) for v in compact
                )
                chosen = (t & (stride - 1)) == jnp.where(low_lanes(32), off_ref[0, level], off_ref[1, level])
                p = jnp.where(chosen, p, -jnp.inf)
                new = jnp.maximum(peak, p)
                fade, weight = jnp.exp(peak - new), jnp.exp(p - new)
                total = total * fade + weight * o
                denom = denom * fade + weight * d
                peak = new
            final[part] = (total / denom).astype(BF)
        part = pl.ds(pl.multiple_of(i * 256, 256), 256)
        both = dot(pick_up[...], final[part])
        rows = jnp.where(low_lanes(64), both[:64], both[64:]).astype(BF)
        late[pl.ds(i * 4, 4)] = rows.reshape(4, 16, WIDE)
        return carry

    lax.fori_loop(0, 4, merge_up, 0)

    def send_late(i, carry):
        to = lax.rem(head + i, HEADS)
        remote(late.at[to], late_in.at[head], late_send, late_recv, seg, to).start()
        return carry

    lax.fori_loop(1, HEADS, send_late, 0)
    late_in[head] = late[head]

    drain(off_tiles.at[pl.ds(0, HEADS - 1)], off_recv)
    drain(early, early_recv)
    drain(late_in.at[pl.ds(0, HEADS - 1)], late_recv)
    t = lax.broadcasted_iota(jnp.int32, (ROWS, WIDE), 0)
    for n in range(HEADS):
        columns = slice(n * WIDE, (n + 1) * WIDE)
        value = early[:, columns].astype(F32)
        rows = late_in[n].astype(F32)
        at = 0
        for level in range(3, 6):
            stride = 1 << level
            count = ROWS >> level
            wide = jnp.concatenate(
                [jnp.broadcast_to(rows[at + k:at + k + 1], (stride, WIDE)) for k in range(count)], axis=0
            )
            value = jnp.where((t & (stride - 1)) == off_tiles[n, level:level + 1], wide, value)
            at += count
        placed[:, columns] = value.astype(BF)
    pltpu.make_async_copy(placed, out_ref, out_sem).start()

    drain(full.at[2, others], in_send.at[2])
    for kv in range(2):
        drain(own1.at[kv], one_send.at[kv])
        drain(gx.at[kv, pl.ds(0, NX - 1)], x_send.at[kv])
        for level in range(3, 6):
            drain(yk.at[kv, level - 3, pl.ds(0, COLUMN_KEYS - rows_of(level))], y_send.at[kv, level - 3])
    drain(qx.at[pl.ds(0, NX - 1)], q_send)
    drain(back_o.at[pl.ds(0, NX - 1)], back_send.at[0])
    drain(back_s.at[pl.ds(0, NX - 1)], back_send.at[1])
    drain(off_tiles.at[pl.ds(0, HEADS - 1)], off_send)
    drain(merged.at[others], early_send)
    drain(late.at[pl.ds(0, HEADS - 1)], late_send)
    drain(out_ref, out_sem)


def per_device(queries, key_states, value_states, offsets):
    dma = pltpu.SemaphoreType.DMA
    hbm = pl.BlockSpec(memory_space=pltpu.HBM)
    return pl.pallas_call(
        kernel,
        out_shape=jax.ShapeDtypeStruct(queries.shape, BF),
        in_specs=[hbm] * 4,
        out_specs=pl.BlockSpec(memory_space=pl.ANY),
        scratch_shapes=[
            pltpu.SMEM((2, 6), jnp.int32),
            pltpu.VMEM((HEADS, 8, WIDE), jnp.int32),
            pltpu.VMEM((512, 256), BF),
            pltpu.VMEM((128, 256), BF),
            pltpu.VMEM((3, BLOCK, WIDE), BF),
            pltpu.VMEM((2, 512, WIDE), BF),
            pltpu.VMEM((2, 512, WIDE), BF),
            pltpu.VMEM((2, NX, 256, WIDE), BF),
            pltpu.VMEM((2, 3, COLUMN_KEYS, WIDE), BF),
            pltpu.VMEM((768, WIDE), BF),
            pltpu.VMEM((NX, UP_ROWS, WIDE), BF),
            pltpu.VMEM((NX, UP_ROWS, WIDE), BF),
            pltpu.VMEM((NX, STAT_ROWS, WIDE), F32),
            pltpu.VMEM((NX, UP_ROWS, WIDE), BF),
            pltpu.VMEM((NX, STAT_ROWS, WIDE), F32),
            pltpu.VMEM((2, BLOCK, WIDE), BF),
        ] + [pltpu.VMEM((BLOCK, WIDE), F32)] * 6 + [pltpu.VMEM((UP_ROWS, WIDE), F32)] * 3 + [
            pltpu.VMEM((BLOCK, WIDE), BF),
            pltpu.VMEM((BLOCK, WIDE), BF),
            pltpu.VMEM((ROWS, D), BF),
            pltpu.VMEM((HEADS, 16, WIDE), BF),
            pltpu.VMEM((HEADS, 16, WIDE), BF),
            pltpu.VMEM((ROWS, D), BF),
            dma, dma, dma, dma((3,)), dma((3,)), dma((2,)), dma((2,)), dma((2,)), dma((2,)), dma((2, 3)), dma((2, 3)),
            dma, dma, dma((2,)), dma((2,)), dma, dma, dma, dma, dma,
        ],
        compiler_params=pltpu.CompilerParams(
            collective_id=0, has_side_effects=True, vmem_limit_bytes=48 * 1024 * 1024
        ),
        cost_estimate=pl.CostEstimate(flops=1100000000, bytes_accessed=1100000, transcendentals=4200000),
    )(*(pltpu.with_memory_space_constraint(a, pltpu.HBM) for a in (offsets, queries, key_states, value_states)))


def solution(mesh):
    rows = P(("seg", "head"), None)
    return jax.shard_map(
        per_device, mesh=mesh, in_specs=(rows, rows, rows, P("head", None)), out_specs=rows, check_vma=False
    )
```

```python
import jax
import jax.numpy as jnp
from jax import lax
from jax.experimental import pallas as pl
from jax.experimental.pallas import tpu as pltpu
from jax.sharding import PartitionSpec as P

MESH = pl.DeviceIdType.MESH
BF = jnp.bfloat16
F32 = jnp.float32

ROWS = 64
BLOCK = 1024
WIDE = 128
HEADS = 16
D = 2048
NX, NY = 4, 8
Q_AT = {1: 0, 2: 512, 3: 768, 4: 896, 5: 960}
UP_AT = {3: 0, 4: 128, 5: 192}
UP_ROWS = 224
COLUMN_KEYS = 256
STAT_ROWS = 32
STAT_GROUPS = UP_ROWS // STAT_ROWS


def rows_of(level):
    return BLOCK >> level


def remote(src, dst, send, recv, seg, head):
    return pltpu.make_async_remote_copy(
        src_ref=src, dst_ref=dst, send_sem=send, recv_sem=recv,
        device_id=(seg, head), device_id_type=MESH,
    )


def drain(ref, sem):
    pltpu.make_async_copy(ref, ref, sem).wait()


def lanes_of(rows):
    return lax.broadcasted_iota(jnp.int32, (rows, WIDE), 1)


def low_lanes(rows):
    return lanes_of(rows) < WIDE // 2


def dot_t(a, b):
    return lax.dot_general(a, b, (((1,), (1,)), ((), ())), preferred_element_type=F32)


def dot(a, b):
    return lax.dot_general(a, b, (((1,), (0,)), ((), ())), preferred_element_type=F32)


def attend(q, k, v_low, v_high):
    rows = q.shape[0]
    low = low_lanes(rows)
    zero = jnp.zeros_like(q)
    q = q * jnp.asarray(0.125, BF)
    both = jnp.concatenate([jnp.where(low, q, zero), jnp.where(low, zero, q)], axis=0)
    scores = dot_t(both, k)
    top = jnp.max(scores, axis=1, keepdims=True)
    probs = jnp.exp(scores - top).astype(BF)
    first = dot(probs[:rows], v_low)
    second = dot(probs[rows:], v_high)
    total = jnp.where(low, first, second)
    denom = pltpu.roll(jnp.where(low, second, first), WIDE // 2, 1)
    return total, denom, jnp.where(low, top[:rows], top[rows:])


def with_ones(v):
    low = low_lanes(v.shape[0])
    one = jnp.ones_like(v)
    return jnp.where(low, v, one), jnp.where(low, one, v)


def kernel(
    off_hbm, q_ref, k_ref, v_ref, out_ref,
    off_ref, off_tiles, q_here, gather_up, up_out, up_in, pick, full, own1, got1, gx, yk, qsel, qx, part_o, part_s, back_o, back_s, v_one,
    acc, den, top, acc_e, den_e, top_e, up_o, up_d, up_t, merged,
    off_sem, q_sem, off_recv, off_send, up_recv, up_send, in_recv, in_send, one_recv, one_send, x_recv, x_send, y_recv, y_send,
    q_recv, q_send, back_recv, back_send, out_recv, out_send,
):
    seg = lax.axis_index("seg")
    head = lax.axis_index("head")
    x = lax.rem(seg, NX)
    y = lax.div(seg, NX)
    offsets = pltpu.make_async_copy(off_hbm, off_ref, off_sem)
    offsets.start()
    queries_here = pltpu.make_async_copy(q_ref, q_here, q_sem)
    queries_here.start()

    barrier = pltpu.get_barrier_semaphore()

    def at_x(i):
        return y * NX + lax.rem(x + i, NX)

    def greet_head(i, carry):
        pl.semaphore_signal(barrier, inc=1, device_id=(seg, lax.rem(head + i, HEADS)), device_id_type=MESH)
        return carry

    def greet_x(i, carry):
        pl.semaphore_signal(barrier, inc=1, device_id=(at_x(i), head), device_id_type=MESH)
        return carry

    def greet_y(i, carry):
        pl.semaphore_signal(barrier, inc=1, device_id=(lax.rem(y + i, NY) * NX + x, head), device_id_type=MESH)
        return carry

    lax.fori_loop(1, HEADS, greet_head, 0)
    lax.fori_loop(1, NX, greet_x, 0)
    lax.fori_loop(1, NY, greet_y, 0)
    pl.semaphore_wait(barrier, (HEADS - 1) + (NX - 1) + (NY - 1))

    mine = pl.ds(pl.multiple_of(head * ROWS, ROWS), ROWS)
    others = pl.ds(0, BLOCK - ROWS)
    my_columns = pl.ds(pl.multiple_of(head * WIDE, WIDE), WIDE)

    def exchange(a):
        ref = (k_ref, v_ref, q_ref)[a]

        def send_in(i, carry):
            to = lax.rem(head + i, HEADS)
            columns = pl.ds(pl.multiple_of(to * WIDE, WIDE), WIDE)
            remote(ref.at[:, columns], full.at[a, mine], in_send.at[a], in_recv.at[a], seg, to).start()
            return carry

        lax.fori_loop(1, HEADS, send_in, 0)
        pltpu.make_async_copy(ref.at[:, my_columns], full.at[a, mine], in_recv.at[a]).start()

    offsets.wait()
    level_row = lax.broadcasted_iota(jnp.int32, (4, WIDE), 0) + 3
    tile = jnp.zeros((4, WIDE), jnp.int32)
    for level in range(3, 6):
        tile = jnp.where(level_row == level, jnp.where(low_lanes(4), off_ref[0, level], off_ref[1, level]), tile)
    off_tiles[head] = tile

    def send_offsets(i, carry):
        to = lax.rem(head + i, HEADS)
        remote(off_tiles.at[head], off_tiles.at[head], off_send, off_recv, seg, to).start()
        return carry

    lax.fori_loop(1, HEADS, send_offsets, 0)
    exchange(0)

    r = lax.broadcasted_iota(jnp.int32, (256, 256), 0)
    c = lax.broadcasted_iota(jnp.int32, (256, 256), 1)
    for h in range(2):
        src = jnp.full((256, 256), -1, jnp.int32)
        at = 248
        for level in range(5, 0, -1):
            at -= 256 >> level
            src = jnp.where(r < at + (256 >> level), ((r - at) << level) + off_ref[h, level], src)
        src = jnp.where(r < 248, src, -1)
        pick[h * 256:(h + 1) * 256] = jnp.where(c == src, 1.0, 0.0).astype(BF)

    r = lax.broadcasted_iota(jnp.int32, (16, 3 * ROWS), 0)
    c = lax.broadcasted_iota(jnp.int32, (16, 3 * ROWS), 1)
    t = c & (ROWS - 1)
    row = jnp.where(c < ROWS, t >> 3, jnp.where(c < 2 * ROWS, 8 + (t >> 4), 12 + (t >> 5)))
    add_up = jnp.where(r == row, 1.0, 0.0).astype(BF)
    r = lax.broadcasted_iota(jnp.int32, (UP_ROWS, HEADS * 16), 0)
    c = lax.broadcasted_iota(jnp.int32, (UP_ROWS, HEADS * 16), 1)
    r4, r5 = r - UP_AT[4], r - UP_AT[5]
    src = jnp.where(
        r < UP_AT[4], ((r >> 3) << 4) + (r & 7),
        jnp.where(r < UP_AT[5], ((r4 >> 2) << 4) + 8 + (r4 & 3), ((r5 >> 1) << 4) + 12 + (r5 & 1)),
    )
    gather_up[...] = jnp.where(c == src, 1.0, 0.0).astype(BF)

    queries_here.wait()
    drain(off_tiles.at[pl.ds(0, HEADS - 1)], off_recv)
    t = lax.broadcasted_iota(jnp.int32, (ROWS, WIDE), 0)
    for n in range(HEADS):
        value = q_here[:, n * WIDE:(n + 1) * WIDE].astype(F32)
        kept = [
            jnp.where((t & ((1 << level) - 1)) == off_tiles[n, level - 3:level - 2], value, 0.0)
            for level in range(3, 6)
        ]
        up_out[n] = dot(add_up, jnp.concatenate(kept, axis=0).astype(BF)).astype(BF)

    def select(a, last):
        count = 256 - (256 >> last) if last < 5 else 256
        low = low_lanes(count)
        chosen = jnp.concatenate([pick[:count], pick[256:256 + count]], axis=0)
        pieces = []
        for n in range(4):
            both = dot(chosen, full[a, n * 256:(n + 1) * 256])
            pieces.append(jnp.where(low, both[:count], both[count:]))
        parts = {}
        at = 0
        for level in range(1, last + 1):
            step = 256 >> level
            parts[level] = jnp.concatenate([piece[at:at + step] for piece in pieces], axis=0).astype(BF)
            at += step
        return parts

    pair = x + 1 - 2 * lax.rem(x, 2)
    partner_x = y * NX + pair
    beside_x = at_x(NX - 1 + 2 * lax.rem(x, 2))

    def start_levels(kv):
        parts = select(kv, 5)
        for level in range(3, 6):
            group = 1 << (level - 2)
            rows = rows_of(level)
            place = lax.rem(y, group)
            slot = yk.at[kv, level - 3, pl.ds(pl.multiple_of(place * rows, rows), rows)]
            slot[...] = parts[level]

            def send_y(i, carry):
                to = y - place + lax.rem(place + i, group)
                remote(slot, slot, y_send.at[kv, level - 3], y_recv.at[kv, level - 3], to * NX + x, head).start()
                return carry

            lax.fori_loop(1, group, send_y, 0)
        own1[kv] = parts[1]
        gx[kv, x] = parts[2]
        held = gx.at[kv, x]
        remote(held, held, x_send.at[kv, 0], x_recv.at[kv, 0], partner_x, head).start()
        remote(held, held, x_send.at[kv, 1], x_recv.at[kv, 1], beside_x, head).start()
        remote(own1.at[kv], got1.at[kv], one_send.at[kv], one_recv.at[kv], partner_x, head).start()

    def pass_on(kv):
        held = gx.at[kv, pair]
        drain(held, x_recv.at[kv, 0])
        remote(held, held, x_send.at[kv, 2], x_recv.at[kv, 2], beside_x, head).start()

    drain(full.at[0, others], in_send.at[0])

    def send_up(i, carry):
        to = lax.rem(head + i, HEADS)
        remote(up_out.at[to], up_in.at[head], up_send, up_recv, seg, to).start()
        return carry

    lax.fori_loop(1, HEADS, send_up, 0)
    up_in[head] = up_out[head]
    exchange(1)
    drain(full.at[0], in_recv.at[0])
    start_levels(0)

    drain(up_in.at[pl.ds(0, HEADS - 1)], up_recv)
    qx[x] = dot(gather_up[...], up_in[...].reshape(HEADS * 16, WIDE)).astype(BF)

    def send_q(i, carry):
        remote(qx.at[x], qx.at[x], q_send, q_recv, at_x(i), head).start()
        return carry

    lax.fori_loop(1, NX, send_q, 0)
    pass_on(0)
    drain(full.at[1, others], in_send.at[1])
    exchange(2)
    drain(full.at[1], in_recv.at[1])
    start_levels(1)
    v_one[0], v_one[1] = with_ones(full[1])
    pass_on(1)

    drain(qx.at[pl.ds(0, NX - 1)], q_recv)
    group_lane = lax.rem(lanes_of(STAT_ROWS), WIDE // 2) // 8
    stats = [jnp.zeros((STAT_ROWS, WIDE), F32) for _ in range(NX)]
    for level in range(3, 6):
        rows = rows_of(level)
        for kv in range(2):
            drain(yk.at[kv, level - 3, pl.ds(0, COLUMN_KEYS - rows)], y_recv.at[kv, level - 3])
        at = UP_AT[level]
        v_low, v_high = with_ones(yk[1, level - 3])
        for n in range(NX):
            total, denom, peak = attend(qx[n, at:at + rows], yk[0, level - 3], v_low, v_high)
            part_o[n, at:at + rows] = (total / denom).astype(BF)
            lse = peak + jnp.log(denom)
            for m in range(rows // STAT_ROWS):
                stats[n] = jnp.where(
                    group_lane == at // STAT_ROWS + m, lse[m * STAT_ROWS:(m + 1) * STAT_ROWS], stats[n]
                )
    for n in range(NX):
        part_s[n] = stats[n]
    back_o[x] = part_o[x]
    back_s[x] = part_s[x]

    def send_back(i, carry):
        to = lax.rem(x + i, NX)
        remote(part_o.at[to], back_o.at[x], back_send.at[0], back_recv.at[0], at_x(i), head).start()
        remote(part_s.at[to], back_s.at[x], back_send.at[1], back_recv.at[1], at_x(i), head).start()
        return carry

    lax.fori_loop(1, NX, send_back, 0)

    drain(full.at[2], in_recv.at[2])
    parts = select(2, 2)
    for level in range(1, 3):
        qsel[Q_AT[level]:Q_AT[level] + rows_of(level)] = parts[level]
    acc[...], den[...], top[...] = attend(full[2], full[0], v_one[0], v_one[1])

    for level in range(1, 3):
        for kv in range(2):
            if level == 1:
                drain(got1.at[kv], one_recv.at[kv])
            else:
                drain(gx.at[kv, 0], x_recv.at[kv, 1])
                drain(gx.at[kv, 0], x_recv.at[kv, 2])
        if level == 1:
            k, v = (jnp.concatenate([own1[kv], got1[kv]], axis=0) for kv in range(2))
        else:
            k, v = (gx[kv].reshape(BLOCK, WIDE) for kv in range(2))
        v_low, v_high = with_ones(v)
        found = attend(qsel[Q_AT[level]:Q_AT[level] + rows_of(level)], k, v_low, v_high)
        stride = 1 << level
        for held, value in zip((acc_e, den_e, top_e), found):
            for o in range(stride):
                held[level - 1, pl.ds(o, rows_of(level), stride=stride), :] = value

    drain(back_o.at[pl.ds(0, NX - 1)], back_recv.at[0])
    drain(back_s.at[pl.ds(0, NX - 1)], back_recv.at[1])
    low = low_lanes(STAT_ROWS)
    for m in range(STAT_GROUPS):
        rows = pl.ds(m * STAT_ROWS, STAT_ROWS)
        lses = []
        for n in range(NX):
            here = jnp.where(group_lane == m, back_s[n], -jnp.inf)
            lses.append(jnp.where(
                low,
                jnp.max(jnp.where(low, here, -jnp.inf), axis=1, keepdims=True),
                jnp.max(jnp.where(low, -jnp.inf, here), axis=1, keepdims=True),
            ))
        peak = jnp.maximum(jnp.maximum(lses[0], lses[1]), jnp.maximum(lses[2], lses[3]))
        weights = [jnp.exp(lse - peak) for lse in lses]
        up_o[rows] = sum(w * back_o[n, rows].astype(F32) for n, w in enumerate(weights))
        up_d[rows] = sum(weights)
        up_t[rows] = peak

    def chosen_rows(rows, level):
        t = lax.broadcasted_iota(jnp.int32, (rows, WIDE), 0)
        return (t & ((1 << level) - 1)) == jnp.where(low_lanes(rows), off_ref[0, level], off_ref[1, level])

    def merge(i, carry):
        quarter = lax.rem(lax.div(head, 4) + i, 4)
        held = {}
        for level in range(3, 6):
            count = 256 >> level
            at = pl.ds(pl.multiple_of(UP_AT[level] + quarter * count, 8), count)
            held[level] = (up_o[at], up_d[at], up_t[at])
        for n in range(8):
            part = pl.ds(pl.multiple_of(quarter * 256 + n * 32, 32), 32)
            total, denom, peak = acc[part], den[part], top[part]
            for level in range(1, 6):
                if level < 3:
                    o, d, p = (e[level - 1, part] for e in (acc_e, den_e, top_e))
                else:
                    count = 32 >> level
                    o, d, p = (
                        jnp.concatenate([
                            jnp.broadcast_to(v[n * count + k:n * count + k + 1], (1 << level, WIDE))
                            for k in range(count)
                        ], axis=0) for v in held[level]
                    )
                p = jnp.where(chosen_rows(32, level), p, -jnp.inf)
                new = jnp.maximum(peak, p)
                fade, weight = jnp.exp(peak - new), jnp.exp(p - new)
                total = total * fade + weight * o
                denom = denom * fade + weight * d
                peak = new
            merged[part] = (total / denom).astype(BF)

        def send_out(k, carry):
            to = quarter * 4 + k

            @pl.when(to != head)
            def _():
                part = pl.ds(pl.multiple_of(to * ROWS, ROWS), ROWS)
                remote(merged.at[part], out_ref.at[:, my_columns], out_send, out_recv, seg, to).start()

            return carry

        lax.fori_loop(0, 4, send_out, 0)
        return carry

    lax.fori_loop(0, 4, merge, 0)
    pltpu.make_async_copy(merged.at[mine], out_ref.at[:, my_columns], out_recv).start()

    drain(full.at[2, others], in_send.at[2])
    for kv in range(2):
        drain(own1.at[kv], one_send.at[kv])
        for n in range(3):
            drain(gx.at[kv, 0], x_send.at[kv, n])
        for level in range(3, 6):
            drain(yk.at[kv, level - 3, pl.ds(0, COLUMN_KEYS - rows_of(level))], y_send.at[kv, level - 3])
    drain(qx.at[pl.ds(0, NX - 1)], q_send)
    drain(back_o.at[pl.ds(0, NX - 1)], back_send.at[0])
    drain(back_s.at[pl.ds(0, NX - 1)], back_send.at[1])
    drain(off_tiles.at[pl.ds(0, HEADS - 1)], off_send)
    drain(up_out.at[pl.ds(0, HEADS - 1)], up_send)
    drain(merged.at[others], out_send)
    drain(out_ref, out_recv)


def per_device(queries, key_states, value_states, offsets):
    dma = pltpu.SemaphoreType.DMA
    hbm = pl.BlockSpec(memory_space=pltpu.HBM)
    return pl.pallas_call(
        kernel,
        out_shape=jax.ShapeDtypeStruct(queries.shape, BF),
        in_specs=[hbm] * 4,
        out_specs=pl.BlockSpec(memory_space=pl.ANY),
        scratch_shapes=[
            pltpu.SMEM((2, 6), jnp.int32),
            pltpu.VMEM((HEADS, 4, WIDE), jnp.int32),
            pltpu.VMEM((ROWS, D), BF),
            pltpu.VMEM((UP_ROWS, HEADS * 16), BF),
            pltpu.VMEM((HEADS, 16, WIDE), BF),
            pltpu.VMEM((HEADS, 16, WIDE), BF),
            pltpu.VMEM((512, 256), BF),
            pltpu.VMEM((3, BLOCK, WIDE), BF),
            pltpu.VMEM((2, 512, WIDE), BF),
            pltpu.VMEM((2, 512, WIDE), BF),
            pltpu.VMEM((2, NX, 256, WIDE), BF),
            pltpu.VMEM((2, 3, COLUMN_KEYS, WIDE), BF),
            pltpu.VMEM((768, WIDE), BF),
            pltpu.VMEM((NX, UP_ROWS, WIDE), BF),
            pltpu.VMEM((NX, UP_ROWS, WIDE), BF),
            pltpu.VMEM((NX, STAT_ROWS, WIDE), F32),
            pltpu.VMEM((NX, UP_ROWS, WIDE), BF),
            pltpu.VMEM((NX, STAT_ROWS, WIDE), F32),
            pltpu.VMEM((2, BLOCK, WIDE), BF),
        ] + [pltpu.VMEM((BLOCK, WIDE), F32)] * 3 + [pltpu.VMEM((2, BLOCK, WIDE), F32)] * 3 + [pltpu.VMEM((UP_ROWS, WIDE), F32)] * 3 + [
            pltpu.VMEM((BLOCK, WIDE), BF),
            dma, dma, dma, dma, dma, dma, dma((3,)), dma((3,)), dma((2,)), dma((2,)), dma((2, 3)), dma((2, 3)), dma((2, 3)), dma((2, 3)),
            dma, dma, dma((2,)), dma((2,)), dma, dma,
        ],
        compiler_params=pltpu.CompilerParams(
            collective_id=0, has_side_effects=True, vmem_limit_bytes=48 * 1024 * 1024
        ),
        cost_estimate=pl.CostEstimate(flops=1100000000, bytes_accessed=1100000, transcendentals=4200000),
    )(*(pltpu.with_memory_space_constraint(a, pltpu.HBM) for a in (offsets, queries, key_states, value_states)))


def solution(mesh):
    rows = P(("seg", "head"), None)
    return jax.shard_map(
        per_device, mesh=mesh, in_specs=(rows, rows, rows, P("head", None)), out_specs=rows, check_vma=False
    )
```

```python
import jax
import jax.numpy as jnp
from jax import lax
from jax.experimental import pallas as pl
from jax.experimental.pallas import tpu as pltpu
from jax.sharding import PartitionSpec as P

MESH = pl.DeviceIdType.MESH
BF = jnp.bfloat16
F32 = jnp.float32

ROWS = 64
BLOCK = 1024
WIDE = 128
HEADS = 16
D = 2048
NX, NY = 4, 8
Q_AT = {1: 0, 2: 512, 3: 768, 4: 896, 5: 960}
UP_AT = {3: 0, 4: 128, 5: 192}
UP_ROWS = 224
COLUMN_KEYS = 256
STAT_ROWS = 32
STAT_GROUPS = UP_ROWS // STAT_ROWS


def rows_of(level):
    return BLOCK >> level


def remote(src, dst, send, recv, seg, head):
    return pltpu.make_async_remote_copy(
        src_ref=src, dst_ref=dst, send_sem=send, recv_sem=recv,
        device_id=(seg, head), device_id_type=MESH,
    )


def drain(ref, sem):
    pltpu.make_async_copy(ref, ref, sem).wait()


def lanes_of(rows):
    return lax.broadcasted_iota(jnp.int32, (rows, WIDE), 1)


def low_lanes(rows):
    return lanes_of(rows) < WIDE // 2


def dot_t(a, b):
    return lax.dot_general(a, b, (((1,), (1,)), ((), ())), preferred_element_type=F32)


def dot(a, b):
    return lax.dot_general(a, b, (((1,), (0,)), ((), ())), preferred_element_type=F32)


def weigh(q, k):
    rows = q.shape[0]
    low = low_lanes(rows)
    zero = jnp.zeros_like(q)
    q = q * jnp.asarray(0.125, BF)
    both = jnp.concatenate([jnp.where(low, q, zero), jnp.where(low, zero, q)], axis=0)
    scores = dot_t(both, k)
    top = jnp.max(scores, axis=1, keepdims=True)
    probs = jnp.exp(scores - top).astype(BF)
    return probs, jnp.where(low, top[:rows], top[rows:])


def add_up_values(probs, v_low, v_high):
    rows = probs.shape[0] // 2
    low = low_lanes(rows)
    first = dot(probs[:rows], v_low)
    second = dot(probs[rows:], v_high)
    total = jnp.where(low, first, second)
    return total, pltpu.roll(jnp.where(low, second, first), WIDE // 2, 1)


def attend(q, k, v_low, v_high):
    probs, top = weigh(q, k)
    return *add_up_values(probs, v_low, v_high), top


def with_ones(v):
    low = low_lanes(v.shape[0])
    one = jnp.ones_like(v)
    return jnp.where(low, v, one), jnp.where(low, one, v)


def kernel(
    off_hbm, q_ref, k_ref, v_ref, out_ref,
    off_ref, off_tiles, q_here, gather_up, up_out, up_in, pick, full, own1, got1, gx, yk, qsel, qx, part_p, part_t, part_o, part_s, back_o, back_s, v_one,
    acc, den, top, acc_e, den_e, top_e, up_o, up_d, up_t, merged,
    off_sem, q_sem, off_recv, off_send, up_recv, up_send, in_recv, in_send, one_recv, one_send, x_recv, x_send, y_recv, y_send,
    q_recv, q_send, back_recv, back_send, out_recv, out_send,
):
    seg = lax.axis_index("seg")
    head = lax.axis_index("head")
    x = lax.rem(seg, NX)
    y = lax.div(seg, NX)
    offsets = pltpu.make_async_copy(off_hbm, off_ref, off_sem)
    offsets.start()
    queries_here = pltpu.make_async_copy(q_ref, q_here, q_sem)
    queries_here.start()

    barrier = pltpu.get_barrier_semaphore()

    def at_x(i):
        return y * NX + lax.rem(x + i, NX)

    def greet_head(i, carry):
        pl.semaphore_signal(barrier, inc=1, device_id=(seg, lax.rem(head + i, HEADS)), device_id_type=MESH)
        return carry

    def greet_x(i, carry):
        pl.semaphore_signal(barrier, inc=1, device_id=(at_x(i), head), device_id_type=MESH)
        return carry

    def greet_y(i, carry):
        pl.semaphore_signal(barrier, inc=1, device_id=(lax.rem(y + i, NY) * NX + x, head), device_id_type=MESH)
        return carry

    lax.fori_loop(1, HEADS, greet_head, 0)
    lax.fori_loop(1, NX, greet_x, 0)
    lax.fori_loop(1, NY, greet_y, 0)
    pl.semaphore_wait(barrier, (HEADS - 1) + (NX - 1) + (NY - 1))

    mine = pl.ds(pl.multiple_of(head * ROWS, ROWS), ROWS)
    others = pl.ds(0, BLOCK - ROWS)
    my_columns = pl.ds(pl.multiple_of(head * WIDE, WIDE), WIDE)

    def exchange(a):
        ref = (k_ref, v_ref, q_ref)[a]

        def send_in(i, carry):
            to = lax.rem(head + HEADS // 2 + lax.div(i, 2) * (1 - 2 * lax.rem(i, 2)), HEADS)
            columns = pl.ds(pl.multiple_of(to * WIDE, WIDE), WIDE)
            remote(ref.at[:, columns], full.at[a, mine], in_send.at[a], in_recv.at[a], seg, to).start()
            return carry

        lax.fori_loop(1, HEADS, send_in, 0)
        pltpu.make_async_copy(ref.at[:, my_columns], full.at[a, mine], in_recv.at[a]).start()

    offsets.wait()
    level_row = lax.broadcasted_iota(jnp.int32, (4, WIDE), 0) + 3
    tile = jnp.zeros((4, WIDE), jnp.int32)
    for level in range(3, 6):
        tile = jnp.where(level_row == level, jnp.where(low_lanes(4), off_ref[0, level], off_ref[1, level]), tile)
    off_tiles[head] = tile

    def send_offsets(i, carry):
        to = lax.rem(head + i, HEADS)
        remote(off_tiles.at[head], off_tiles.at[head], off_send, off_recv, seg, to).start()
        return carry

    lax.fori_loop(1, HEADS, send_offsets, 0)
    exchange(0)

    r = lax.broadcasted_iota(jnp.int32, (256, 256), 0)
    c = lax.broadcasted_iota(jnp.int32, (256, 256), 1)
    for h in range(2):
        src = jnp.full((256, 256), -1, jnp.int32)
        at = 248
        for level in range(5, 0, -1):
            at -= 256 >> level
            src = jnp.where(r < at + (256 >> level), ((r - at) << level) + off_ref[h, level], src)
        src = jnp.where(r < 248, src, -1)
        pick[h * 256:(h + 1) * 256] = jnp.where(c == src, 1.0, 0.0).astype(BF)

    r = lax.broadcasted_iota(jnp.int32, (16, 3 * ROWS), 0)
    c = lax.broadcasted_iota(jnp.int32, (16, 3 * ROWS), 1)
    t = c & (ROWS - 1)
    row = jnp.where(c < ROWS, t >> 3, jnp.where(c < 2 * ROWS, 8 + (t >> 4), 12 + (t >> 5)))
    add_up = jnp.where(r == row, 1.0, 0.0).astype(BF)
    r = lax.broadcasted_iota(jnp.int32, (UP_ROWS, HEADS * 16), 0)
    c = lax.broadcasted_iota(jnp.int32, (UP_ROWS, HEADS * 16), 1)
    r4, r5 = r - UP_AT[4], r - UP_AT[5]
    src = jnp.where(
        r < UP_AT[4], ((r >> 3) << 4) + (r & 7),
        jnp.where(r < UP_AT[5], ((r4 >> 2) << 4) + 8 + (r4 & 3), ((r5 >> 1) << 4) + 12 + (r5 & 1)),
    )
    gather_up[...] = jnp.where(c == src, 1.0, 0.0).astype(BF)

    queries_here.wait()
    drain(off_tiles.at[pl.ds(0, HEADS - 1)], off_recv)
    t = lax.broadcasted_iota(jnp.int32, (ROWS, WIDE), 0)
    for n in range(HEADS):
        value = q_here[:, n * WIDE:(n + 1) * WIDE].astype(F32)
        kept = [
            jnp.where((t & ((1 << level) - 1)) == off_tiles[n, level - 3:level - 2], value, 0.0)
            for level in range(3, 6)
        ]
        up_out[n] = dot(add_up, jnp.concatenate(kept, axis=0).astype(BF)).astype(BF)

    def select(a, last):
        count = 256 - (256 >> last) if last < 5 else 256
        low = low_lanes(count)
        chosen = jnp.concatenate([pick[:count], pick[256:256 + count]], axis=0)
        pieces = []
        for n in range(4):
            both = dot(chosen, full[a, n * 256:(n + 1) * 256])
            pieces.append(jnp.where(low, both[:count], both[count:]))
        parts = {}
        at = 0
        for level in range(1, last + 1):
            step = 256 >> level
            parts[level] = jnp.concatenate([piece[at:at + step] for piece in pieces], axis=0).astype(BF)
            at += step
        return parts

    pair = x + 1 - 2 * lax.rem(x, 2)
    partner_x = y * NX + pair
    beside_x = at_x(NX - 1 + 2 * lax.rem(x, 2))

    def start_levels(kv):
        parts = select(kv, 5)
        for level in range(3, 6):
            group = 1 << (level - 2)
            rows = rows_of(level)
            place = lax.rem(y, group)
            slot = yk.at[kv, level - 3, pl.ds(pl.multiple_of(place * rows, rows), rows)]
            slot[...] = parts[level]

            def send_y(i, carry):
                to = y - place + lax.rem(place + i, group)
                remote(slot, slot, y_send.at[kv, level - 3], y_recv.at[kv, level - 3], to * NX + x, head).start()
                return carry

            lax.fori_loop(1, group, send_y, 0)
        own1[kv] = parts[1]
        gx[kv, x] = parts[2]
        held = gx.at[kv, x]
        remote(held, held, x_send.at[kv, 0], x_recv.at[kv, 0], partner_x, head).start()
        remote(held, held, x_send.at[kv, 1], x_recv.at[kv, 1], beside_x, head).start()
        remote(own1.at[kv], got1.at[kv], one_send.at[kv], one_recv.at[kv], partner_x, head).start()

    def pass_on(kv):
        held = gx.at[kv, pair]
        drain(held, x_recv.at[kv, 0])
        remote(held, held, x_send.at[kv, 2], x_recv.at[kv, 2], beside_x, head).start()

    drain(full.at[0, others], in_send.at[0])

    def send_up(i, carry):
        to = lax.rem(head + i, HEADS)
        remote(up_out.at[to], up_in.at[head], up_send, up_recv, seg, to).start()
        return carry

    lax.fori_loop(1, HEADS, send_up, 0)
    up_in[head] = up_out[head]
    exchange(1)
    drain(full.at[0], in_recv.at[0])
    start_levels(0)

    drain(up_in.at[pl.ds(0, HEADS - 1)], up_recv)
    qx[x] = dot(gather_up[...], up_in[...].reshape(HEADS * 16, WIDE)).astype(BF)

    def send_q(i, carry):
        remote(qx.at[x], qx.at[x], q_send, q_recv, at_x(i), head).start()
        return carry

    lax.fori_loop(1, NX, send_q, 0)
    pass_on(0)
    drain(full.at[1, others], in_send.at[1])
    exchange(2)
    drain(full.at[1], in_recv.at[1])
    start_levels(1)
    v_one[0], v_one[1] = with_ones(full[1])
    pass_on(1)

    drain(qx.at[pl.ds(0, NX - 1)], q_recv)
    for level in range(3, 6):
        rows, at = rows_of(level), UP_AT[level]
        drain(yk.at[0, level - 3, pl.ds(0, COLUMN_KEYS - rows)], y_recv.at[0, level - 3])
        for n in range(NX):
            part_p[n, 2 * at:2 * (at + rows)], part_t[n, at:at + rows] = weigh(qx[n, at:at + rows], yk[0, level - 3])
    group_lane = lax.rem(lanes_of(STAT_ROWS), WIDE // 2) // 8
    stats = [jnp.zeros((STAT_ROWS, WIDE), F32) for _ in range(NX)]
    for level in range(3, 6):
        rows, at = rows_of(level), UP_AT[level]
        drain(yk.at[1, level - 3, pl.ds(0, COLUMN_KEYS - rows)], y_recv.at[1, level - 3])
        v_low, v_high = with_ones(yk[1, level - 3])
        for n in range(NX):
            total, denom = add_up_values(part_p[n, 2 * at:2 * (at + rows)], v_low, v_high)
            part_o[n, at:at + rows] = (total / denom).astype(BF)
            lse = part_t[n, at:at + rows] + jnp.log(denom)
            for m in range(rows // STAT_ROWS):
                stats[n] = jnp.where(
                    group_lane == at // STAT_ROWS + m, lse[m * STAT_ROWS:(m + 1) * STAT_ROWS], stats[n]
                )
    for n in range(NX):
        part_s[n] = stats[n]
    back_o[x] = part_o[x]
    back_s[x] = part_s[x]

    def send_back(i, carry):
        to = lax.rem(x + i, NX)
        remote(part_o.at[to], back_o.at[x], back_send.at[0], back_recv.at[0], at_x(i), head).start()
        remote(part_s.at[to], back_s.at[x], back_send.at[1], back_recv.at[1], at_x(i), head).start()
        return carry

    lax.fori_loop(1, NX, send_back, 0)

    drain(full.at[2], in_recv.at[2])
    parts = select(2, 2)
    for level in range(1, 3):
        qsel[Q_AT[level]:Q_AT[level] + rows_of(level)] = parts[level]
    acc[...], den[...], top[...] = attend(full[2], full[0], v_one[0], v_one[1])

    for level in range(1, 3):
        for kv in range(2):
            if level == 1:
                drain(got1.at[kv], one_recv.at[kv])
            else:
                drain(gx.at[kv, 0], x_recv.at[kv, 1])
                drain(gx.at[kv, 0], x_recv.at[kv, 2])
        if level == 1:
            k, v = (jnp.concatenate([own1[kv], got1[kv]], axis=0) for kv in range(2))
        else:
            k, v = (gx[kv].reshape(BLOCK, WIDE) for kv in range(2))
        v_low, v_high = with_ones(v)
        found = attend(qsel[Q_AT[level]:Q_AT[level] + rows_of(level)], k, v_low, v_high)
        stride = 1 << level
        for held, value in zip((acc_e, den_e, top_e), found):
            for o in range(stride):
                held[level - 1, pl.ds(o, rows_of(level), stride=stride), :] = value

    drain(back_o.at[pl.ds(0, NX - 1)], back_recv.at[0])
    drain(back_s.at[pl.ds(0, NX - 1)], back_recv.at[1])
    low = low_lanes(STAT_ROWS)
    for m in range(STAT_GROUPS):
        rows = pl.ds(m * STAT_ROWS, STAT_ROWS)
        lses = []
        for n in range(NX):
            here = jnp.where(group_lane == m, back_s[n], -jnp.inf)
            lses.append(jnp.where(
                low,
                jnp.max(jnp.where(low, here, -jnp.inf), axis=1, keepdims=True),
                jnp.max(jnp.where(low, -jnp.inf, here), axis=1, keepdims=True),
            ))
        peak = jnp.maximum(jnp.maximum(lses[0], lses[1]), jnp.maximum(lses[2], lses[3]))
        weights = [jnp.exp(lse - peak) for lse in lses]
        up_o[rows] = sum(w * back_o[n, rows].astype(F32) for n, w in enumerate(weights))
        up_d[rows] = sum(weights)
        up_t[rows] = peak

    def chosen_rows(rows, level):
        t = lax.broadcasted_iota(jnp.int32, (rows, WIDE), 0)
        return (t & ((1 << level) - 1)) == jnp.where(low_lanes(rows), off_ref[0, level], off_ref[1, level])

    def merge(i, carry):
        quarter = lax.rem(lax.div(head, 4) + 2 + i, 4)
        held = {}
        for level in range(3, 6):
            count = 256 >> level
            at = pl.ds(pl.multiple_of(UP_AT[level] + quarter * count, 8), count)
            held[level] = (up_o[at], up_d[at], up_t[at])
        for n in range(8):
            part = pl.ds(pl.multiple_of(quarter * 256 + n * 32, 32), 32)
            total, denom, peak = acc[part], den[part], top[part]
            for level in range(1, 6):
                if level < 3:
                    o, d, p = (e[level - 1, part] for e in (acc_e, den_e, top_e))
                else:
                    count = 32 >> level
                    o, d, p = (
                        jnp.concatenate([
                            jnp.broadcast_to(v[n * count + k:n * count + k + 1], (1 << level, WIDE))
                            for k in range(count)
                        ], axis=0) for v in held[level]
                    )
                p = jnp.where(chosen_rows(32, level), p, -jnp.inf)
                new = jnp.maximum(peak, p)
                fade, weight = jnp.exp(peak - new), jnp.exp(p - new)
                total = total * fade + weight * o
                denom = denom * fade + weight * d
                peak = new
            merged[part] = (total / denom).astype(BF)

        def send_out(k, carry):
            to = quarter * 4 + k

            @pl.when(to != head)
            def _():
                part = pl.ds(pl.multiple_of(to * ROWS, ROWS), ROWS)
                remote(merged.at[part], out_ref.at[:, my_columns], out_send, out_recv, seg, to).start()

            return carry

        lax.fori_loop(0, 4, send_out, 0)
        return carry

    lax.fori_loop(0, 4, merge, 0)
    pltpu.make_async_copy(merged.at[mine], out_ref.at[:, my_columns], out_recv).start()

    drain(full.at[2, others], in_send.at[2])
    for kv in range(2):
        drain(own1.at[kv], one_send.at[kv])
        for n in range(3):
            drain(gx.at[kv, 0], x_send.at[kv, n])
        for level in range(3, 6):
            drain(yk.at[kv, level - 3, pl.ds(0, COLUMN_KEYS - rows_of(level))], y_send.at[kv, level - 3])
    drain(qx.at[pl.ds(0, NX - 1)], q_send)
    drain(back_o.at[pl.ds(0, NX - 1)], back_send.at[0])
    drain(back_s.at[pl.ds(0, NX - 1)], back_send.at[1])
    drain(off_tiles.at[pl.ds(0, HEADS - 1)], off_send)
    drain(up_out.at[pl.ds(0, HEADS - 1)], up_send)
    drain(merged.at[others], out_send)
    drain(out_ref, out_recv)


def per_device(queries, key_states, value_states, offsets):
    dma = pltpu.SemaphoreType.DMA
    hbm = pl.BlockSpec(memory_space=pltpu.HBM)
    return pl.pallas_call(
        kernel,
        out_shape=jax.ShapeDtypeStruct(queries.shape, BF),
        in_specs=[hbm] * 4,
        out_specs=pl.BlockSpec(memory_space=pl.ANY),
        scratch_shapes=[
            pltpu.SMEM((2, 6), jnp.int32),
            pltpu.VMEM((HEADS, 4, WIDE), jnp.int32),
            pltpu.VMEM((ROWS, D), BF),
            pltpu.VMEM((UP_ROWS, HEADS * 16), BF),
            pltpu.VMEM((HEADS, 16, WIDE), BF),
            pltpu.VMEM((HEADS, 16, WIDE), BF),
            pltpu.VMEM((512, 256), BF),
            pltpu.VMEM((3, BLOCK, WIDE), BF),
            pltpu.VMEM((2, 512, WIDE), BF),
            pltpu.VMEM((2, 512, WIDE), BF),
            pltpu.VMEM((2, NX, 256, WIDE), BF),
            pltpu.VMEM((2, 3, COLUMN_KEYS, WIDE), BF),
            pltpu.VMEM((768, WIDE), BF),
            pltpu.VMEM((NX, UP_ROWS, WIDE), BF),
            pltpu.VMEM((NX, 2 * UP_ROWS, COLUMN_KEYS), BF),
            pltpu.VMEM((NX, UP_ROWS, WIDE), F32),
            pltpu.VMEM((NX, UP_ROWS, WIDE), BF),
            pltpu.VMEM((NX, STAT_ROWS, WIDE), F32),
            pltpu.VMEM((NX, UP_ROWS, WIDE), BF),
            pltpu.VMEM((NX, STAT_ROWS, WIDE), F32),
            pltpu.VMEM((2, BLOCK, WIDE), BF),
        ] + [pltpu.VMEM((BLOCK, WIDE), F32)] * 3 + [pltpu.VMEM((2, BLOCK, WIDE), F32)] * 3 + [pltpu.VMEM((UP_ROWS, WIDE), F32)] * 3 + [
            pltpu.VMEM((BLOCK, WIDE), BF),
            dma, dma, dma, dma, dma, dma, dma((3,)), dma((3,)), dma((2,)), dma((2,)), dma((2, 3)), dma((2, 3)), dma((2, 3)), dma((2, 3)),
            dma, dma, dma((2,)), dma((2,)), dma, dma,
        ],
        compiler_params=pltpu.CompilerParams(
            collective_id=0, has_side_effects=True, vmem_limit_bytes=48 * 1024 * 1024
        ),
        cost_estimate=pl.CostEstimate(flops=1100000000, bytes_accessed=1100000, transcendentals=4200000),
    )(*(pltpu.with_memory_space_constraint(a, pltpu.HBM) for a in (offsets, queries, key_states, value_states)))


def solution(mesh):
    rows = P(("seg", "head"), None)
    return jax.shard_map(
        per_device, mesh=mesh, in_specs=(rows, rows, rows, P("head", None)), out_specs=rows, check_vma=False
    )
```

```python
import jax
import jax.numpy as jnp
from jax import lax
from jax.experimental import pallas as pl
from jax.experimental.pallas import tpu as pltpu
from jax.sharding import PartitionSpec as P

MESH = pl.DeviceIdType.MESH
BF = jnp.bfloat16
F32 = jnp.float32

ROWS = 64
BLOCK = 1024
WIDE = 128
HEADS = 16
D = 2048
NX, NY = 4, 8
Q_AT = {1: 0, 2: 512, 3: 768, 4: 896, 5: 960}
UP_AT = {3: 0, 4: 128, 5: 192}
UP_ROWS = 224
COLUMN_KEYS = 256
STAT_ROWS = 32
STAT_GROUPS = UP_ROWS // STAT_ROWS


def rows_of(level):
    return BLOCK >> level


def remote(src, dst, send, recv, seg, head):
    return pltpu.make_async_remote_copy(
        src_ref=src, dst_ref=dst, send_sem=send, recv_sem=recv,
        device_id=(seg, head), device_id_type=MESH,
    )


def drain(ref, sem):
    pltpu.make_async_copy(ref, ref, sem).wait()


def lanes_of(rows):
    return lax.broadcasted_iota(jnp.int32, (rows, WIDE), 1)


def low_lanes(rows):
    return lanes_of(rows) < WIDE // 2


def dot_t(a, b):
    return lax.dot_general(a, b, (((1,), (1,)), ((), ())), preferred_element_type=F32)


def dot(a, b):
    return lax.dot_general(a, b, (((1,), (0,)), ((), ())), preferred_element_type=F32)


def weigh(q, k):
    rows = q.shape[0]
    low = low_lanes(rows)
    zero = jnp.zeros_like(q)
    q = q * jnp.asarray(0.125, BF)
    both = jnp.concatenate([jnp.where(low, q, zero), jnp.where(low, zero, q)], axis=0)
    scores = dot_t(both, k)
    top = jnp.max(scores, axis=1, keepdims=True)
    probs = jnp.exp(scores - top).astype(BF)
    return probs, jnp.where(low, top[:rows], top[rows:])


def add_up_values(probs, v_low, v_high):
    rows = probs.shape[0] // 2
    low = low_lanes(rows)
    first = dot(probs[:rows], v_low)
    second = dot(probs[rows:], v_high)
    total = jnp.where(low, first, second)
    return total, pltpu.roll(jnp.where(low, second, first), WIDE // 2, 1)


def attend(q, k, v_low, v_high):
    probs, top = weigh(q, k)
    return *add_up_values(probs, v_low, v_high), top


def with_ones(v):
    low = low_lanes(v.shape[0])
    one = jnp.ones_like(v)
    return jnp.where(low, v, one), jnp.where(low, one, v)


def kernel(
    off_hbm, q_ref, k_ref, v_ref, out_ref,
    off_ref, off_tiles, q_here, gather_up, up_out, up_in, pick, full, own1, got1, gx, yk, qsel, qx, part_p, part_t, part_o, part_s, back_o, back_s, v_one,
    acc, den, top, acc_e, den_e, top_e, up_o, up_d, up_t, merged,
    off_sem, q_sem, off_recv, off_send, up_recv, up_send, in_recv, in_send, one_recv, one_send, x_recv, x_send, y_recv, y_send,
    q_recv, q_send, back_recv, back_send, out_recv, out_send,
):
    seg = lax.axis_index("seg")
    head = lax.axis_index("head")
    x = lax.rem(seg, NX)
    y = lax.div(seg, NX)
    offsets = pltpu.make_async_copy(off_hbm, off_ref, off_sem)
    offsets.start()
    queries_here = pltpu.make_async_copy(q_ref, q_here, q_sem)
    queries_here.start()

    barrier = pltpu.get_barrier_semaphore()

    def at_x(i):
        return y * NX + lax.rem(x + i, NX)

    def greet_head(i, carry):
        pl.semaphore_signal(barrier, inc=1, device_id=(seg, lax.rem(head + i, HEADS)), device_id_type=MESH)
        return carry

    def greet_x(i, carry):
        pl.semaphore_signal(barrier, inc=1, device_id=(at_x(i), head), device_id_type=MESH)
        return carry

    def greet_y(i, carry):
        pl.semaphore_signal(barrier, inc=1, device_id=(lax.rem(y + i, NY) * NX + x, head), device_id_type=MESH)
        return carry

    lax.fori_loop(1, HEADS, greet_head, 0)
    lax.fori_loop(1, NX, greet_x, 0)
    lax.fori_loop(1, NY, greet_y, 0)
    pl.semaphore_wait(barrier, (HEADS - 1) + (NX - 1) + (NY - 1))

    mine = pl.ds(pl.multiple_of(head * ROWS, ROWS), ROWS)
    others = pl.ds(0, BLOCK - ROWS)
    my_columns = pl.ds(pl.multiple_of(head * WIDE, WIDE), WIDE)

    def exchange(a):
        ref = (k_ref, v_ref, q_ref)[a]

        def send_in(i, carry):
            to = lax.rem(head + HEADS // 2 + lax.div(i, 2) * (1 - 2 * lax.rem(i, 2)), HEADS)
            columns = pl.ds(pl.multiple_of(to * WIDE, WIDE), WIDE)
            remote(ref.at[:, columns], full.at[a, mine], in_send.at[a], in_recv.at[a], seg, to).start()
            return carry

        lax.fori_loop(1, HEADS, send_in, 0)
        pltpu.make_async_copy(ref.at[:, my_columns], full.at[a, mine], in_recv.at[a]).start()

    offsets.wait()
    level_row = lax.broadcasted_iota(jnp.int32, (4, WIDE), 0) + 3
    tile = jnp.zeros((4, WIDE), jnp.int32)
    for level in range(3, 6):
        tile = jnp.where(level_row == level, jnp.where(low_lanes(4), off_ref[0, level], off_ref[1, level]), tile)
    off_tiles[head] = tile

    def send_offsets(i, carry):
        to = lax.rem(head + HEADS // 2 + lax.div(i, 2) * (1 - 2 * lax.rem(i, 2)), HEADS)
        remote(off_tiles.at[head], off_tiles.at[head], off_send, off_recv, seg, to).start()
        return carry

    lax.fori_loop(1, HEADS, send_offsets, 0)
    exchange(0)

    r = lax.broadcasted_iota(jnp.int32, (256, 256), 0)
    c = lax.broadcasted_iota(jnp.int32, (256, 256), 1)
    for h in range(2):
        src = jnp.full((256, 256), -1, jnp.int32)
        at = 248
        for level in range(5, 0, -1):
            at -= 256 >> level
            src = jnp.where(r < at + (256 >> level), ((r - at) << level) + off_ref[h, level], src)
        src = jnp.where(r < 248, src, -1)
        pick[h * 256:(h + 1) * 256] = jnp.where(c == src, 1.0, 0.0).astype(BF)

    r = lax.broadcasted_iota(jnp.int32, (16, 3 * ROWS), 0)
    c = lax.broadcasted_iota(jnp.int32, (16, 3 * ROWS), 1)
    t = c & (ROWS - 1)
    row = jnp.where(c < ROWS, t >> 3, jnp.where(c < 2 * ROWS, 8 + (t >> 4), 12 + (t >> 5)))
    add_up = jnp.where(r == row, 1.0, 0.0).astype(BF)
    r = lax.broadcasted_iota(jnp.int32, (UP_ROWS, HEADS * 16), 0)
    c = lax.broadcasted_iota(jnp.int32, (UP_ROWS, HEADS * 16), 1)
    r4, r5 = r - UP_AT[4], r - UP_AT[5]
    src = jnp.where(
        r < UP_AT[4], ((r >> 3) << 4) + (r & 7),
        jnp.where(r < UP_AT[5], ((r4 >> 2) << 4) + 8 + (r4 & 3), ((r5 >> 1) << 4) + 12 + (r5 & 1)),
    )
    gather_up[...] = jnp.where(c == src, 1.0, 0.0).astype(BF)

    queries_here.wait()
    drain(off_tiles.at[pl.ds(0, HEADS - 1)], off_recv)
    t = lax.broadcasted_iota(jnp.int32, (ROWS, WIDE), 0)
    for n in range(HEADS):
        value = q_here[:, n * WIDE:(n + 1) * WIDE].astype(F32)
        kept = [
            jnp.where((t & ((1 << level) - 1)) == off_tiles[n, level - 3:level - 2], value, 0.0)
            for level in range(3, 6)
        ]
        up_out[n] = dot(add_up, jnp.concatenate(kept, axis=0).astype(BF)).astype(BF)

    def select(a, last):
        count = 256 - (256 >> last) if last < 5 else 256
        low = low_lanes(count)
        chosen = jnp.concatenate([pick[:count], pick[256:256 + count]], axis=0)
        pieces = []
        for n in range(4):
            both = dot(chosen, full[a, n * 256:(n + 1) * 256])
            pieces.append(jnp.where(low, both[:count], both[count:]))
        parts = {}
        at = 0
        for level in range(1, last + 1):
            step = 256 >> level
            parts[level] = jnp.concatenate([piece[at:at + step] for piece in pieces], axis=0).astype(BF)
            at += step
        return parts

    pair = x + 1 - 2 * lax.rem(x, 2)
    partner_x = y * NX + pair
    beside_x = at_x(NX - 1 + 2 * lax.rem(x, 2))

    def start_levels(kv):
        parts = select(kv, 5)
        for level in range(3, 6):
            group = 1 << (level - 2)
            rows = rows_of(level)
            place = lax.rem(y, group)
            slot = yk.at[kv, level - 3, pl.ds(pl.multiple_of(place * rows, rows), rows)]
            slot[...] = parts[level]

            def send_y(i, carry):
                to = y - place + lax.rem(place + i, group)
                remote(slot, slot, y_send.at[kv, level - 3], y_recv.at[kv, level - 3], to * NX + x, head).start()
                return carry

            lax.fori_loop(1, group, send_y, 0)
        own1[kv] = parts[1]
        gx[kv, x] = parts[2]
        held = gx.at[kv, x]
        remote(held, held, x_send.at[kv, 0], x_recv.at[kv, 0], partner_x, head).start()
        remote(held, held, x_send.at[kv, 1], x_recv.at[kv, 1], beside_x, head).start()
        remote(own1.at[kv], got1.at[kv], one_send.at[kv], one_recv.at[kv], partner_x, head).start()

    def pass_on(kv):
        held = gx.at[kv, pair]
        drain(held, x_recv.at[kv, 0])
        remote(held, held, x_send.at[kv, 2], x_recv.at[kv, 2], beside_x, head).start()

    drain(full.at[0, others], in_send.at[0])

    def send_up(i, carry):
        to = lax.rem(head + HEADS // 2 + lax.div(i, 2) * (1 - 2 * lax.rem(i, 2)), HEADS)
        remote(up_out.at[to], up_in.at[head], up_send, up_recv, seg, to).start()
        return carry

    lax.fori_loop(1, HEADS, send_up, 0)
    up_in[head] = up_out[head]
    exchange(1)
    drain(full.at[0], in_recv.at[0])
    start_levels(0)

    drain(up_in.at[pl.ds(0, HEADS - 1)], up_recv)
    qx[x] = dot(gather_up[...], up_in[...].reshape(HEADS * 16, WIDE)).astype(BF)

    def send_q(i, carry):
        remote(qx.at[x], qx.at[x], q_send, q_recv, at_x(i), head).start()
        return carry

    lax.fori_loop(1, NX, send_q, 0)
    pass_on(0)
    drain(full.at[1, others], in_send.at[1])
    exchange(2)
    drain(full.at[1], in_recv.at[1])
    start_levels(1)
    v_one[0], v_one[1] = with_ones(full[1])
    pass_on(1)

    drain(qx.at[pl.ds(0, NX - 1)], q_recv)
    for level in range(3, 6):
        rows, at = rows_of(level), UP_AT[level]
        drain(yk.at[0, level - 3, pl.ds(0, COLUMN_KEYS - rows)], y_recv.at[0, level - 3])
        for n in range(NX):
            part_p[n, 2 * at:2 * (at + rows)], part_t[n, at:at + rows] = weigh(qx[n, at:at + rows], yk[0, level - 3])
    group_lane = lax.rem(lanes_of(STAT_ROWS), WIDE // 2) // 8
    stats = [jnp.zeros((STAT_ROWS, WIDE), F32) for _ in range(NX)]
    for level in range(3, 6):
        rows, at = rows_of(level), UP_AT[level]
        drain(yk.at[1, level - 3, pl.ds(0, COLUMN_KEYS - rows)], y_recv.at[1, level - 3])
        v_low, v_high = with_ones(yk[1, level - 3])
        for n in range(NX):
            total, denom = add_up_values(part_p[n, 2 * at:2 * (at + rows)], v_low, v_high)
            part_o[n, at:at + rows] = (total / denom).astype(BF)
            lse = part_t[n, at:at + rows] + jnp.log(denom)
            for m in range(rows // STAT_ROWS):
                stats[n] = jnp.where(
                    group_lane == at // STAT_ROWS + m, lse[m * STAT_ROWS:(m + 1) * STAT_ROWS], stats[n]
                )
    for n in range(NX):
        part_s[n] = stats[n]
    back_o[x] = part_o[x]
    back_s[x] = part_s[x]

    def send_back(i, carry):
        to = lax.rem(x + i, NX)
        remote(part_o.at[to], back_o.at[x], back_send.at[0], back_recv.at[0], at_x(i), head).start()
        remote(part_s.at[to], back_s.at[x], back_send.at[1], back_recv.at[1], at_x(i), head).start()
        return carry

    lax.fori_loop(1, NX, send_back, 0)

    drain(full.at[2], in_recv.at[2])
    parts = select(2, 2)
    for level in range(1, 3):
        qsel[Q_AT[level]:Q_AT[level] + rows_of(level)] = parts[level]
    acc[...], den[...], top[...] = attend(full[2], full[0], v_one[0], v_one[1])

    for level in range(1, 3):
        for kv in range(2):
            if level == 1:
                drain(got1.at[kv], one_recv.at[kv])
            else:
                drain(gx.at[kv, 0], x_recv.at[kv, 1])
                drain(gx.at[kv, 0], x_recv.at[kv, 2])
        if level == 1:
            k, v = (jnp.concatenate([own1[kv], got1[kv]], axis=0) for kv in range(2))
        else:
            k, v = (gx[kv].reshape(BLOCK, WIDE) for kv in range(2))
        v_low, v_high = with_ones(v)
        found = attend(qsel[Q_AT[level]:Q_AT[level] + rows_of(level)], k, v_low, v_high)
        stride = 1 << level
        for held, value in zip((acc_e, den_e, top_e), found):
            for o in range(stride):
                held[level - 1, pl.ds(o, rows_of(level), stride=stride), :] = value

    drain(back_o.at[pl.ds(0, NX - 1)], back_recv.at[0])
    drain(back_s.at[pl.ds(0, NX - 1)], back_recv.at[1])
    low = low_lanes(STAT_ROWS)
    for m in range(STAT_GROUPS):
        rows = pl.ds(m * STAT_ROWS, STAT_ROWS)
        lses = []
        for n in range(NX):
            here = jnp.where(group_lane == m, back_s[n], -jnp.inf)
            lses.append(jnp.where(
                low,
                jnp.max(jnp.where(low, here, -jnp.inf), axis=1, keepdims=True),
                jnp.max(jnp.where(low, -jnp.inf, here), axis=1, keepdims=True),
            ))
        peak = jnp.maximum(jnp.maximum(lses[0], lses[1]), jnp.maximum(lses[2], lses[3]))
        weights = [jnp.exp(lse - peak) for lse in lses]
        up_o[rows] = sum(w * back_o[n, rows].astype(F32) for n, w in enumerate(weights))
        up_d[rows] = sum(weights)
        up_t[rows] = peak

    def chosen_rows(rows, level):
        t = lax.broadcasted_iota(jnp.int32, (rows, WIDE), 0)
        return (t & ((1 << level) - 1)) == jnp.where(low_lanes(rows), off_ref[0, level], off_ref[1, level])

    def merge(i, carry):
        apart = 2 + lax.div(i + 1, 2) * (2 * lax.rem(i + 1, 2) - 1)
        quarter = lax.rem(lax.div(head, 4) + apart, 4)
        held = {}
        for level in range(3, 6):
            count = 256 >> level
            at = pl.ds(pl.multiple_of(UP_AT[level] + quarter * count, 8), count)
            held[level] = (up_o[at], up_d[at], up_t[at])
        for n in range(8):
            part = pl.ds(pl.multiple_of(quarter * 256 + n * 32, 32), 32)
            total, denom, peak = acc[part], den[part], top[part]
            for level in range(1, 6):
                if level < 3:
                    o, d, p = (e[level - 1, part] for e in (acc_e, den_e, top_e))
                else:
                    count = 32 >> level
                    o, d, p = (
                        jnp.concatenate([
                            jnp.broadcast_to(v[n * count + k:n * count + k + 1], (1 << level, WIDE))
                            for k in range(count)
                        ], axis=0) for v in held[level]
                    )
                p = jnp.where(chosen_rows(32, level), p, -jnp.inf)
                new = jnp.maximum(peak, p)
                fade, weight = jnp.exp(peak - new), jnp.exp(p - new)
                total = total * fade + weight * o
                denom = denom * fade + weight * d
                peak = new
            merged[part] = (total / denom).astype(BF)

        def send_out(k, carry):
            to = quarter * 4 + k

            @pl.when(to != head)
            def _():
                part = pl.ds(pl.multiple_of(to * ROWS, ROWS), ROWS)
                remote(merged.at[part], out_ref.at[:, my_columns], out_send, out_recv, seg, to).start()

            return carry

        lax.fori_loop(0, 4, send_out, 0)
        return carry

    lax.fori_loop(0, 4, merge, 0)
    pltpu.make_async_copy(merged.at[mine], out_ref.at[:, my_columns], out_recv).start()

    drain(full.at[2, others], in_send.at[2])
    for kv in range(2):
        drain(own1.at[kv], one_send.at[kv])
        for n in range(3):
            drain(gx.at[kv, 0], x_send.at[kv, n])
        for level in range(3, 6):
            drain(yk.at[kv, level - 3, pl.ds(0, COLUMN_KEYS - rows_of(level))], y_send.at[kv, level - 3])
    drain(qx.at[pl.ds(0, NX - 1)], q_send)
    drain(back_o.at[pl.ds(0, NX - 1)], back_send.at[0])
    drain(back_s.at[pl.ds(0, NX - 1)], back_send.at[1])
    drain(off_tiles.at[pl.ds(0, HEADS - 1)], off_send)
    drain(up_out.at[pl.ds(0, HEADS - 1)], up_send)
    drain(merged.at[others], out_send)
    drain(out_ref, out_recv)


def per_device(queries, key_states, value_states, offsets):
    dma = pltpu.SemaphoreType.DMA
    hbm = pl.BlockSpec(memory_space=pltpu.HBM)
    return pl.pallas_call(
        kernel,
        out_shape=jax.ShapeDtypeStruct(queries.shape, BF),
        in_specs=[hbm] * 4,
        out_specs=pl.BlockSpec(memory_space=pl.ANY),
        scratch_shapes=[
            pltpu.SMEM((2, 6), jnp.int32),
            pltpu.VMEM((HEADS, 4, WIDE), jnp.int32),
            pltpu.VMEM((ROWS, D), BF),
            pltpu.VMEM((UP_ROWS, HEADS * 16), BF),
            pltpu.VMEM((HEADS, 16, WIDE), BF),
            pltpu.VMEM((HEADS, 16, WIDE), BF),
            pltpu.VMEM((512, 256), BF),
            pltpu.VMEM((3, BLOCK, WIDE), BF),
            pltpu.VMEM((2, 512, WIDE), BF),
            pltpu.VMEM((2, 512, WIDE), BF),
            pltpu.VMEM((2, NX, 256, WIDE), BF),
            pltpu.VMEM((2, 3, COLUMN_KEYS, WIDE), BF),
            pltpu.VMEM((768, WIDE), BF),
            pltpu.VMEM((NX, UP_ROWS, WIDE), BF),
            pltpu.VMEM((NX, 2 * UP_ROWS, COLUMN_KEYS), BF),
            pltpu.VMEM((NX, UP_ROWS, WIDE), F32),
            pltpu.VMEM((NX, UP_ROWS, WIDE), BF),
            pltpu.VMEM((NX, STAT_ROWS, WIDE), F32),
            pltpu.VMEM((NX, UP_ROWS, WIDE), BF),
            pltpu.VMEM((NX, STAT_ROWS, WIDE), F32),
            pltpu.VMEM((2, BLOCK, WIDE), BF),
        ] + [pltpu.VMEM((BLOCK, WIDE), F32)] * 3 + [pltpu.VMEM((2, BLOCK, WIDE), F32)] * 3 + [pltpu.VMEM((UP_ROWS, WIDE), F32)] * 3 + [
            pltpu.VMEM((BLOCK, WIDE), BF),
            dma, dma, dma, dma, dma, dma, dma((3,)), dma((3,)), dma((2,)), dma((2,)), dma((2, 3)), dma((2, 3)), dma((2, 3)), dma((2, 3)),
            dma, dma, dma((2,)), dma((2,)), dma, dma,
        ],
        compiler_params=pltpu.CompilerParams(
            collective_id=0, has_side_effects=True, vmem_limit_bytes=48 * 1024 * 1024
        ),
        cost_estimate=pl.CostEstimate(flops=1100000000, bytes_accessed=1100000, transcendentals=4200000),
    )(*(pltpu.with_memory_space_constraint(a, pltpu.HBM) for a in (offsets, queries, key_states, value_states)))


def solution(mesh):
    rows = P(("seg", "head"), None)
    return jax.shard_map(
        per_device, mesh=mesh, in_specs=(rows, rows, rows, P("head", None)), out_specs=rows, check_vma=False
    )
```
